256 devices in a mesh: ctx: 16 (over z, core), exp: 16 (over x, y).
Axes of the slice: x: 4, y: 4, z: 8, core: 2. Of those that a mesh axis runs over, the one named last changes fastest.
Arguments:
- q_pref: bfloat16 [2048, 128, 576], P('ctx', 'exp'), may hold values from -10 to 10
- kv_pref: bfloat16 [2048, 576], P('ctx'), may hold values from -4 to 4
- dec_q: bfloat16 [256, 128, 576], P('exp', 'ctx'), may hold values from -10 to 10
- dec_kv: bfloat16 [256, 576], P('exp'), may hold values from -4 to 4
- page_req: int32 [16, 16], P('exp'), may hold values from 0 to 127, as said below
- dec_len: int32 [256], P('exp'), may hold values from 1 to 256, as said below
- w_uv: bfloat16 [128, 512, 128], P('ctx'), may hold values from -1 to 1
- w_o: bfloat16 [16384, 7168], P('ctx', 'exp'), may hold values from -0.09375 to 0.09375
- x_dec: bfloat16 [256, 7168], P('exp'), may hold values from -6 to 6
- norm_gain: bfloat16 [7168], replicated, may hold values from 0.5 to 1.5
- router: bfloat16 [7168, 16], replicated, may hold values from -0.0625 to 0.0625
- routes: int32 [256, 8], P('exp'), may hold values from 0 to 15, all different within a row; in each aligned block of 16 rows (0 to 15, 16 to 31, ...) at most 10 rows name the same one
- w_gate: bfloat16 [16, 7168, 2048], P('exp', None, 'ctx'), may hold values from -0.0625 to 0.0625
- w_up: bfloat16 [16, 7168, 2048], P('exp', None, 'ctx'), may hold values from -0.0625 to 0.0625
- w_down: bfloat16 [16, 2048, 7168], P('exp', 'ctx'), may hold values from -0.125 to 0.125
Outputs:
- pref_out: bfloat16 [2048, 128, 512], P('ctx', 'exp')
- decode_out: bfloat16 [256, 7168], P('exp')
The draws below stay inside these ranges and needn't reach their ends.
Inputs may be any that keep to these rules, and one draw needn't show every extreme that they name: `page_req`: entries of one list differ. Pages i * 8 to (i + 1) * 8 - 1 belong to index i of ctx; a list names at most 2 pages of one index, and every list names exactly 2 pages of some index. `dec_len`: every index of exp holds a row whose length is 256. `routes`: each row names 8 different experts; the rows of one index of exp name one expert at most 10 times.
All inputs are finite; a program needn't handle non-finite values.
Results may differ from the reference program's by a relative error of at most 0.019.
Values may be sent and summed in bfloat16 or wider, within the bound.
A program may use at most 192 MiB of HBM per device.

```python
import math
import jax
import jax.numpy as jnp
import numpy as np
from jax import lax

D = 7168
KVL = 512
HEADS = 128
VD = 128
FFE = 2048
TOPK = 8
EXPERTS = 16
PAGE = 16
CAPP = 2
TOK_DEV = 128
DR_DEV = 16
LAT = 576
SEQ = 2048
DROWS = 256
REQ = 16
CAPE = 10
N_CTX = 16
N_EXP = 16


def key_material(key, row_count, salt):
    gaussian = jax.random.normal(jax.random.fold_in(key, salt), (row_count, LAT), jnp.float32)
    return gaussian


def request_pages(key):
    key = jax.random.fold_in(key, 31)
    item_count = N_CTX * CAPP
    per_source = TOK_DEV // PAGE
    item_owner = jnp.arange(item_count) // CAPP

    def one_group(group_key):
        order_key, force_key, offset_key, mix_key = jax.random.split(group_key, 4)
        rank_order = jax.random.permutation(order_key, item_count)
        forced = jax.random.randint(force_key, (), 0, N_CTX)
        priority = jnp.where(item_owner == forced, rank_order - item_count, rank_order)
        taken_items = jnp.argsort(priority)[:N_CTX]
        taken_items = taken_items[jax.random.permutation(mix_key, N_CTX)]
        offsets = jax.random.randint(offset_key, (N_CTX,), 0, per_source)
        source = taken_items // CAPP
        return (source * per_source + (offsets[source] + taken_items % CAPP) % per_source).astype(jnp.int32)
    return jax.vmap(one_group)(jax.random.split(key, N_EXP))


def draw_kv_pref(key, part):
    gaussian = key_material(key, SEQ, 11)
    return jnp.clip(gaussian, -4.0, 4.0).astype(jnp.bfloat16)


def draw_dec_kv(key, part):
    gaussian = key_material(key, DROWS, 21)
    return jnp.clip(gaussian, -4.0, 4.0).astype(jnp.bfloat16)


def draw_page_req(key, part):
    return request_pages(key)


def draw_dec_len(key, part):
    key = jax.random.fold_in(key, 4)
    row_lengths = jax.random.randint(key, (DROWS,), 1, REQ * PAGE + 1)
    full_row = jax.random.randint(jax.random.fold_in(key, 9), (N_EXP,), 0, DR_DEV)
    row_index = jnp.arange(DROWS)
    return jnp.where(row_index % DR_DEV == full_row[row_index // DR_DEV], REQ * PAGE, row_lengths).astype(jnp.int32)


def draw_q_pref(key, part):
    key = jax.random.fold_in(key, 5)
    return jnp.clip(jax.random.normal(key, (SEQ, HEADS, LAT), jnp.float32), -4.0, 4.0).astype(jnp.bfloat16)


def draw_dec_q(key, part):
    key = jax.random.fold_in(key, 6)
    return jnp.clip(jax.random.normal(key, (DROWS, HEADS, LAT), jnp.float32), -4.0, 4.0).astype(jnp.bfloat16)


def block_levels(rng, shape, pieces, smallest, high):
    gain = 1.0
    for axis_at, parts in pieces:
        steps = jax.random.uniform(jax.random.fold_in(jax.random.fold_in(rng, 6), axis_at), (parts,), jnp.float32, smallest / len(pieces), high / len(pieces))
        gain = gain * jnp.repeat(jnp.exp(steps), shape[axis_at] // parts).reshape((-1,) + (1,) * (len(shape) - 1 - axis_at))
    return gain


def routed_block(key, own, number, rows, count, top, most, lean):
    ranking = jax.random.permutation(key, count)
    packed, common = shares(count, rows * top, most, lean, True), shares(count, rows * top, most, lean, False)
    places = jnp.arange(count)

    def named(sizes, offset_by):
        used = int((sizes > 0).sum())
        fixed = max(1, used // 4)
        shifted = fixed + (places - fixed + offset_by * (used - fixed)) % max(1, count - fixed)
        return jnp.zeros((count,), jnp.int32).at[ranking[jnp.where(places < fixed, places, shifted)]].set(jnp.asarray(sizes, jnp.int32))

    sizes = jnp.where(number % 4 == 0, named(packed, number // 4), named(common, number - number // 4 - 1))
    mixed = jax.random.permutation(jax.random.fold_in(own, 3), count)
    donor, taker = mixed[0:count // 2 * 2:2], mixed[1:count // 2 * 2:2]
    margin = jnp.minimum(sizes[donor] - 1, most - sizes[taker]) // 2
    margin = jnp.where((donor == ranking[0]) | (taker == ranking[0]) | (sizes[taker] == 0), 0, jnp.maximum(margin, 0))
    shifted = jax.random.randint(jax.random.fold_in(own, 4), (count // 2,), 0, 1 << 20) % (margin + 1)
    sizes = sizes.at[donor].add(-shifted).at[taker].add(shifted)
    labels = jnp.searchsorted(jnp.cumsum(sizes), jnp.arange(rows * top), side="right").astype(jnp.int32)
    table = labels.reshape(top, rows).T
    table = table[jax.random.permutation(jax.random.fold_in(own, 1), rows)]
    offset_by = jax.random.randint(jax.random.fold_in(own, 2), (rows, 1), 0, top)
    return jnp.take_along_axis(table, (jnp.arange(top)[None, :] + offset_by) % top, axis=1)


def shares(number_of, total, limit, skew, full):
    weights = [(1 << 20) // math.isqrt(grade ** skew) + 1 for grade in range(1, number_of + 1)]
    largest = limit if full else min(limit, max(-(-total // number_of), total * weights[0] // sum(weights)))
    least = 1 if total - largest >= number_of - 1 else 0
    holding, surplus = [largest] + [least] * (number_of - 1), total - largest - least * (number_of - 1)
    while surplus > 0:
        candidates = [i for i in range(1, number_of) if holding[i] < largest] or [i for i in range(1, number_of) if holding[i] < limit]
        pool, remaining = sum([weights[i] for i in candidates]), surplus
        for i in candidates:
            addition = min(limit - holding[i], max(1, remaining * weights[i] // pool), surplus)
            holding[i] = holding[i] + addition
            surplus = surplus - addition
    return np.array(holding)


def bell_draw(rng, shape, width, limit, cuts=(), held_as=jnp.bfloat16):
    array = jax.random.normal(rng, shape, jnp.float32) * width
    if len(cuts) > 0:
        array = block_levels(rng, shape, cuts, -0.22, 0.18) * array
    return jnp.clip(array, min=-limit, max=limit).astype(held_as)


def setup_inputs(seed: int = 0) -> dict:
    splits = jax.random.split(jax.random.key(seed), 16)
    q_pref = draw_q_pref(jax.random.fold_in(splits[15], 71), 0)
    kv_pref = draw_kv_pref(jax.random.fold_in(splits[15], 71), 0)
    dec_q = draw_dec_q(jax.random.fold_in(splits[15], 71), 0)
    dec_kv = draw_dec_kv(jax.random.fold_in(splits[15], 71), 0)
    page_req = draw_page_req(jax.random.fold_in(splits[15], 71), 0)
    dec_len = draw_dec_len(jax.random.fold_in(splits[15], 71), 0)
    w_uv = bell_draw(splits[6], (HEADS, KVL, VD), (KVL // 16) ** -0.5, 1.0, ((0, 16),))
    w_o = bell_draw(splits[7], (HEADS * VD, D), (HEADS * VD // 4) ** -0.5, 0.09375, ((0, 16), (1, 16)))
    x_dec = bell_draw(splits[8], (DROWS, D), 1.0, 6.0, ((0, 16),))
    norm_gain = jnp.clip(1.0 + 0.1 * jax.random.normal(splits[9], (D,), jnp.float32), 0.5, 1.5).astype(jnp.bfloat16)
    router = bell_draw(splits[10], (D, EXPERTS), D ** -0.5, 0.0625)
    routes_keys = jax.random.split(jax.random.fold_in(splits[11], 1), DROWS // DR_DEV)
    routes_turns = jax.random.permutation(jax.random.fold_in(splits[11], 3), DROWS // DR_DEV)
    routes = jax.vmap(lambda own, number: routed_block(jax.random.fold_in(splits[11], 2), own, number, DR_DEV, EXPERTS, TOPK, CAPE, 2))(routes_keys, routes_turns).reshape((DROWS, TOPK))
    w_gate = bell_draw(splits[12], (EXPERTS, D, FFE), D ** -0.5, 0.0625, ((0, 16), (2, 16)))
    w_up = bell_draw(splits[13], (EXPERTS, D, FFE), D ** -0.5, 0.0625, ((0, 16), (2, 16)))
    w_down = bell_draw(splits[14], (EXPERTS, FFE, D), FFE ** -0.5, 0.125, ((0, 16), (1, 16)))
    return dict(q_pref=q_pref, kv_pref=kv_pref, dec_q=dec_q, dec_kv=dec_kv, page_req=page_req, dec_len=dec_len, w_uv=w_uv, w_o=w_o, x_dec=x_dec, norm_gain=norm_gain, router=router, routes=routes, w_gate=w_gate, w_up=w_up, w_down=w_down)


qk_scale = 192.0 ** (-0.5)
neg_big = -1e+30

def reference(q_pref, kv_pref, dec_q, dec_kv, page_req, dec_len, w_uv, w_o, x_dec, norm_gain, router, routes, w_gate, w_up, w_down):
    block_rows = min(128, SEQ)
    key_rows = kv_pref.astype(jnp.float32)
    value_rows = key_rows[:, :KVL]
    key_pos = jnp.arange(SEQ)

    def prefill(q_index):
        first_row = q_index * block_rows
        query_rows = lax.dynamic_slice_in_dim(q_pref, first_row, block_rows, 0).astype(jnp.float32)
        scores = jnp.einsum('thc,kc->thk', query_rows, key_rows) * qk_scale
        allowed = key_pos[None, None, :] <= (first_row + jnp.arange(block_rows))[:, None, None]
        row_max = lax.optimization_barrier(jnp.max(jnp.where(allowed, scores, neg_big), axis=2, keepdims=True))
        weights = jnp.where(allowed, jnp.exp(scores - row_max), 0.0)
        weight_sum = lax.optimization_barrier(jnp.sum(weights, axis=2, keepdims=True))
        rounded = lax.optimization_barrier(weights.astype(jnp.bfloat16)).astype(jnp.float32)
        return (jnp.einsum('thk,kc->thc', rounded, value_rows) / weight_sum).astype(jnp.bfloat16)
    pref_out = lax.map(prefill, jnp.arange(SEQ // block_rows)).reshape(SEQ, HEADS, KVL)
    page_rows = kv_pref.reshape(SEQ // PAGE, PAGE * LAT)
    key_cache = page_rows[page_req].reshape(N_EXP, REQ * PAGE, LAT).astype(jnp.float32)
    queries = dec_q.reshape(N_EXP, DR_DEV, HEADS, LAT).astype(jnp.float32)
    own_keys = dec_kv.reshape(N_EXP, DR_DEV, LAT).astype(jnp.float32)
    scores = jnp.einsum('grhc,gkc->grhk', queries, key_cache) * qk_scale
    own_score = jnp.einsum('grhc,grc->grh', queries, own_keys) * qk_scale
    lengths = dec_len.reshape(N_EXP, DR_DEV)
    allowed = jnp.arange(REQ * PAGE)[None, None, None, :] < lengths[:, :, None, None]
    row_max = jnp.maximum(lax.optimization_barrier(jnp.max(jnp.where(allowed, scores, neg_big), axis=3)), own_score)
    weights = jnp.where(allowed, jnp.exp(scores - row_max[..., None]), 0.0)
    own_weight = jnp.exp(own_score - row_max)
    weight_sum = lax.optimization_barrier(jnp.sum(weights, axis=3)) + own_weight
    rounded = lax.optimization_barrier(weights.astype(jnp.bfloat16)).astype(jnp.float32)
    own_round = lax.optimization_barrier(own_weight.astype(jnp.bfloat16)).astype(jnp.float32)
    mixed_sum = jnp.einsum('grhk,gkc->grhc', rounded, key_cache[..., :KVL]) + own_round[..., None] * own_keys[:, :, None, :KVL]
    dec_lat = (mixed_sum / weight_sum[..., None]).astype(jnp.bfloat16).reshape(DROWS, HEADS, KVL)
    head_vals = jnp.einsum('rhc,hcv->rhv', dec_lat.astype(jnp.float32), w_uv.astype(jnp.float32)).astype(jnp.bfloat16)
    head_out = jnp.dot(head_vals.reshape(DROWS, HEADS * VD), w_o, preferred_element_type=jnp.float32)
    residual = x_dec.astype(jnp.float32) + head_out
    normed = (residual * lax.rsqrt(lax.optimization_barrier(jnp.mean(residual * residual, axis=-1, keepdims=True)) + 1e-06) * norm_gain.astype(jnp.float32)).astype(jnp.bfloat16)
    affinity = jax.nn.sigmoid(jnp.dot(normed, router, preferred_element_type=jnp.float32))
    chosen = routes[:, :, None] == jnp.arange(EXPERTS)[None, None, :]
    picked = lax.optimization_barrier(jnp.sum(jnp.where(chosen, affinity[:, None, :], 0.0), axis=2))
    gate_share = 2.5 * picked / lax.optimization_barrier(jnp.sum(picked, axis=1, keepdims=True))
    per_expert = lax.optimization_barrier(jnp.sum(jnp.where(chosen, gate_share[:, :, None], 0.0), axis=1))

    def expert(running, expert_item):
        gate_w, up_w, down_w, row_share = expert_item
        gate_val = jnp.dot(normed, gate_w, preferred_element_type=jnp.float32)
        up_val = jnp.dot(normed, up_w, preferred_element_type=jnp.float32)
        hidden = (jax.nn.silu(gate_val) * up_val).astype(jnp.bfloat16)
        return (running + row_share[:, None] * jnp.dot(hidden, down_w, preferred_element_type=jnp.float32), None)
    routed_sum, _ = lax.scan(expert, jnp.zeros((DROWS, D), jnp.float32), (w_gate, w_up, w_down, per_expert.T))
    decode_out = (residual + routed_sum).astype(jnp.bfloat16)
    return (pref_out, decode_out)
```

```python
import functools

import jax
import jax.numpy as jnp
from jax import lax
from jax.experimental import pallas as pl
from jax.experimental.pallas import tpu as pltpu
from jax.sharding import PartitionSpec as P

D = 7168
HALF = D // 2
KVL = 512
LAT = 576
HEADS_DEV = 8
VD = 128
FF = 128
TOK = 128
PAGE = 16
GROUP = 16
COLS = 448
EXT = 128
WIDE = HALF + EXT
PIECE = 512

qk_scale = 192.0 ** (-0.5)
neg_big = -1e30
MESH = pl.DeviceIdType.MESH
VMEM = pltpu.VMEM
ANY = pl.ANY
LIMIT = 56 * 1024 * 1024


class Place:
    def __init__(self):
        self.c = lax.axis_index("ctx")
        self.e = lax.axis_index("exp")
        self.z, self.k = self.c // 2, self.c % 2
        x, y = self.e // 4, self.e % 4
        self.a = x + self.k * (y - x)
        self.b = y + self.k * (x - y)

    def exp_of(self, a, b):
        return (a + self.k * (b - a)) * 4 + b + self.k * (a - b)

    def plane(self, a, b):
        return (self.c, self.exp_of(a % 4, b % 4))

    def sibling(self):
        return (self.c + 1 - 2 * self.k, self.e)

    def along_z(self, step):
        return (((self.z + step) % 8) * 2 + self.k, self.e)


def greet(devices):
    barrier = pltpu.get_barrier_semaphore()
    for device in devices:
        pl.semaphore_signal(barrier, inc=1, device_id=device, device_id_type=MESH)
    pl.semaphore_wait(barrier, len(devices))


class Wires:
    def __init__(self, send_sem, recv_sem):
        self.send_sem, self.recv_sem = send_sem, recv_sem
        self.count = 0
        self.open = []

    def copy(self, src, dst, device):
        i = self.count
        self.count += 1
        made = pltpu.make_async_remote_copy(
            src_ref=src,
            dst_ref=dst,
            send_sem=self.send_sem.at[i],
            recv_sem=self.recv_sem.at[i],
            device_id=device,
            device_id_type=MESH,
        )
        made.start()
        self.open.append(made)
        return made

    def drain(self):
        for made in self.open:
            made.wait_send()
        self.open = []


def plane_gather(place, wires, buf, first):
    a, b = place.a, place.b
    lo, hi = pl.ds(0, first), pl.ds(first, buf.shape[2] - first)

    def slot(i, j):
        return (j % 4) * 4 + i % 4

    def both(ref, right, left):
        return wires.copy(ref, ref, right), wires.copy(ref, ref, left)

    def relay(i, j, i2, j2, right, left, got):
        got[0].wait_recv()
        one = buf.at[slot(i, j), :, lo]
        first_half = wires.copy(one, one, right)
        got[1].wait_recv()
        two = buf.at[slot(i2, j2), :, hi]
        return first_half, wires.copy(two, two, left)

    a_right, a_left = place.plane(a + 1, b), place.plane(a - 1, b)
    b_right, b_left = place.plane(a, b + 1), place.plane(a, b - 1)
    mine = buf.at[slot(a, b)]
    near = both(mine, a_right, a_left)
    columns = [(0, both(mine, b_right, b_left))]
    far = relay(a - 1, b, a + 1, b, a_right, a_left, near)
    for step in (-1, 1):
        ref = buf.at[slot(a + step, b)]
        columns.append((step, both(ref, b_right, b_left)))
    halves = []
    for step, got in columns[:2]:
        halves.append(relay(a + step, b - 1, a + step, b + 1, b_right, b_left, got))
    far[0].wait_recv()
    far[1].wait_recv()
    ref = buf.at[slot(a + 2, b)]
    columns.append((2, both(ref, b_right, b_left)))
    for step, got in columns[2:]:
        halves.append(relay(a + step, b - 1, a + step, b + 1, b_right, b_left, got))

    def finish():
        for one, two in halves:
            one.wait_recv()
            two.wait_recv()

    return finish


GATHER_COPIES = 20


def ring_sum(wires, right, left, piece, rx1r, rx1l, t_r, t_l, rx2r, rx2l, first):
    far = piece(2)
    lo, hi = pl.ds(0, first), pl.ds(first, far.shape[-1] - first)
    one = wires.copy(far.at[..., lo], rx1r, right)
    two = wires.copy(far.at[..., hi], rx1l, left)
    one.wait_recv()
    near = piece(1)
    t_r[..., hi] = near[..., hi]
    t_r[..., lo] = (near[..., lo].astype(jnp.float32) + rx1r[...].astype(jnp.float32)).astype(
        jnp.bfloat16
    )
    three = wires.copy(t_r, rx2r, right)
    two.wait_recv()
    near = piece(-1)
    t_l[..., lo] = near[..., lo]
    t_l[..., hi] = (near[..., hi].astype(jnp.float32) + rx1l[...].astype(jnp.float32)).astype(
        jnp.bfloat16
    )
    four = wires.copy(t_l, rx2l, left)
    three.wait_recv()
    four.wait_recv()
    return (
        piece(0)[...].astype(jnp.float32)
        + rx2r[...].astype(jnp.float32)
        + rx2l[...].astype(jnp.float32)
    )


def keys_kernel(kv, gate, up, down, keys, s_gate, s_up, s_down, send, recv, here):
    place = Place()
    z, k = place.z, place.k
    sibling, right, left = place.sibling(), place.along_z(1), place.along_z(-1)
    greet([sibling, right, left])
    wires = Wires(send, recv)

    def slot(step):
        return ((z + step) % 8) * 2 + k

    mine = keys.at[slot(0)]
    to_r = wires.copy(kv, mine, right)
    to_l = wires.copy(kv, mine, left)
    from_sibling = [wires.copy(kv, mine, sibling)]
    local = pltpu.make_async_copy(kv, mine, here)
    local.start()
    other = pl.ds((1 - k) * HALF, HALF)
    swaps = [
        wires.copy(gate.at[0, other, :], s_gate, sibling),
        wires.copy(up.at[0, other, :], s_up, sibling),
        wires.copy(down.at[0, :, other], s_down, sibling),
    ]
    for hop in (1, 2, 3):
        to_r.wait_recv()
        ref = keys.at[slot(-hop)]
        part = ref if hop < 3 else keys.at[slot(-hop), pl.ds(0, TOK // 2), :]
        to_r = wires.copy(part, part, right)
        from_sibling.append(wires.copy(ref, ref, sibling))
        to_l.wait_recv()
        ref = keys.at[slot(hop)]
        part = ref if hop < 3 else keys.at[slot(hop), pl.ds(TOK // 2, TOK // 2), :]
        to_l = wires.copy(part, part, left)
        from_sibling.append(wires.copy(ref, ref, sibling))
    to_r.wait_recv()
    to_l.wait_recv()
    ref = keys.at[slot(4)]
    from_sibling.append(wires.copy(ref, ref, sibling))
    for made in from_sibling + swaps:
        made.wait_recv()
    local.wait()
    wires.drain()


def gather_keys(kv, w_gate, w_up, w_down):
    copies = 2 + 1 + 3 + 3 * 4 + 1
    return pl.pallas_call(
        keys_kernel,
        out_shape=(
            jax.ShapeDtypeStruct((16, TOK, LAT), jnp.bfloat16),
            jax.ShapeDtypeStruct((HALF, FF), jnp.bfloat16),
            jax.ShapeDtypeStruct((HALF, FF), jnp.bfloat16),
            jax.ShapeDtypeStruct((FF, HALF), jnp.bfloat16),
        ),
        in_specs=[pl.BlockSpec(memory_space=ANY)] * 4,
        out_specs=[pl.BlockSpec(memory_space=ANY)] * 4,
        scratch_shapes=[
            pltpu.SemaphoreType.DMA((copies,)),
            pltpu.SemaphoreType.DMA((copies,)),
            pltpu.SemaphoreType.DMA,
        ],
        compiler_params=pltpu.CompilerParams(collective_id=1, has_side_effects=True),
    )(kv, w_gate, w_up, w_down)


def prefill_kernel(q, keys, out):
    rows = q.shape[0] * HEADS_DEV
    c = lax.axis_index("ctx")
    queries = q[...].reshape(rows, LAT)
    scores = lax.dot_general(
        queries, keys[...], (((1,), (1,)), ((), ())), preferred_element_type=jnp.float32
    )
    first = c * TOK + pl.program_id(0) * q.shape[0]
    token = first + lax.broadcasted_iota(jnp.int32, (rows, 1), 0) // HEADS_DEV
    key = lax.broadcasted_iota(jnp.int32, scores.shape, 1)
    scores = jnp.where(key <= token, scores, neg_big)
    top = jnp.max(scores, axis=1, keepdims=True)
    weights = jnp.exp((scores - top) * qk_scale)
    total = jnp.sum(weights, axis=1, keepdims=True)
    mixed = jnp.dot(
        weights.astype(jnp.bfloat16), keys[:, :KVL], preferred_element_type=jnp.float32
    )
    out[...] = (mixed / total).astype(jnp.bfloat16).reshape(out.shape)


def prefill(q, keys):
    tile = 32
    return pl.pallas_call(
        prefill_kernel,
        grid=(q.shape[0] // tile,),
        out_shape=jax.ShapeDtypeStruct((q.shape[0], HEADS_DEV, KVL), jnp.bfloat16),
        in_specs=[
            pl.BlockSpec((tile, HEADS_DEV, LAT), lambda i: (i, 0, 0)),
            pl.BlockSpec(keys.shape, lambda i: (0, 0)),
        ],
        out_specs=pl.BlockSpec((tile, HEADS_DEV, KVL), lambda i: (i, 0, 0)),
        compiler_params=pltpu.CompilerParams(vmem_limit_bytes=LIMIT),
    )(q, keys)


def decode_kernel(pages, lengths, q, own, keys, w_uv, vals, cache, sem):
    copies = []
    for i in range(16):
        page = pages[0, i]
        made = pltpu.make_async_copy(keys.at[page], cache.at[i], sem.at[i])
        made.start()
        copies.append(made)
    rows = HEADS_DEV * GROUP
    queries = q[...].reshape(rows, LAT)
    own_all = jnp.broadcast_to(own[...][None], (HEADS_DEV, GROUP, LAT)).reshape(rows, LAT)
    own_all = own_all.astype(jnp.float32)
    own_score = jnp.sum(queries.astype(jnp.float32) * own_all, axis=1, keepdims=True)
    for made in copies:
        made.wait()
    cached = cache[...].reshape(16 * PAGE, LAT)
    scores = lax.dot_general(
        queries, cached, (((1,), (1,)), ((), ())), preferred_element_type=jnp.float32
    )
    row = lax.broadcasted_iota(jnp.int32, (rows, 1), 0) % GROUP
    limit = jnp.zeros((rows, 1), jnp.int32)
    for i in range(GROUP):
        limit = jnp.where(row == i, lengths[i], limit)
    allowed = lax.broadcasted_iota(jnp.int32, scores.shape, 1) < limit
    scores = jnp.where(allowed, scores, neg_big)
    top = jnp.maximum(jnp.max(scores, axis=1, keepdims=True), own_score)
    weights = jnp.where(allowed, jnp.exp((scores - top) * qk_scale), 0.0)
    own_weight = jnp.exp((own_score - top) * qk_scale)
    total = jnp.sum(weights, axis=1, keepdims=True) + own_weight
    mixed = jnp.dot(
        weights.astype(jnp.bfloat16), cached[:, :KVL], preferred_element_type=jnp.float32
    )
    mixed = mixed + own_weight.astype(jnp.bfloat16).astype(jnp.float32) * own_all[:, :KVL]
    latent = (mixed / total).astype(jnp.bfloat16)
    for h in range(HEADS_DEV):
        part = jnp.dot(
            latent[h * GROUP : (h + 1) * GROUP], w_uv[h], preferred_element_type=jnp.float32
        )
        vals[:, h * VD : (h + 1) * VD] = part.astype(jnp.bfloat16)


def decode_attention(pages, lengths, q, own, keys, w_uv):
    vmem = pl.BlockSpec(memory_space=VMEM)
    smem = pl.BlockSpec(memory_space=pltpu.SMEM)
    return pl.pallas_call(
        decode_kernel,
        out_shape=jax.ShapeDtypeStruct((GROUP, HEADS_DEV * VD), jnp.bfloat16),
        in_specs=[smem, smem, vmem, vmem, pl.BlockSpec(memory_space=ANY), vmem],
        out_specs=vmem,
        scratch_shapes=[
            VMEM((16, PAGE, LAT), jnp.bfloat16),
            pltpu.SemaphoreType.DMA((16,)),
        ],
        compiler_params=pltpu.CompilerParams(vmem_limit_bytes=LIMIT),
    )(pages, lengths, q, own, keys, w_uv)


def project_kernel(
    vals, w_o, out, rows, part, rx_sib, red, rx_z, groups, arrived, send, recv, send2, recv2
):
    place = Place()
    z, k, a, b, c, e = place.z, place.k, place.a, place.b, place.c, place.e
    sibling = place.sibling()
    partners = [sibling] + [place.along_z(d) for d in range(1, 8)]
    for i in range(1, 16):
        other = (e + i) % 16
        partners.append((2 * z, other))
        partners.append((2 * z + 1, other))
    greet(partners)
    wires = Wires(send, recv)
    rows[b * 4 + a] = vals[...]
    finish = plane_gather(place, wires, rows, rows.shape[2] // 2)
    finish()
    product = jnp.dot(
        rows[...].reshape(256, rows.shape[2]), w_o[...], preferred_element_type=jnp.float32
    )
    for s in range(16):
        part[place.exp_of(s % 4, s // 4)] = product[s * 16 : s * 16 + 16].astype(jnp.bfloat16)
    swap = wires.copy(part.at[pl.ds((1 - k) * 8, 8)], rx_sib, sibling)
    swap.wait_recv()
    red[...] = (
        part[pl.ds(k * 8, 8)].astype(jnp.float32) + rx_sib[...].astype(jnp.float32)
    ).astype(jnp.bfloat16)
    spread = []
    for d in range(1, 8):
        spread.append(wires.copy(red.at[(z + d) % 8], rx_z.at[d - 1], place.along_z(d)))
    total = red[z].astype(jnp.float32)
    for d in range(1, 8):
        spread[d - 1].wait_recv()
        total = total + rx_z[d - 1].astype(jnp.float32)
    groups[z] = total.astype(jnp.bfloat16)
    shared = []
    for d in range(1, 8):
        shared.append(wires.copy(groups.at[z], groups.at[z], place.along_z(d)))

    def hand_over(t, core):
        return pltpu.make_async_remote_copy(
            src_ref=groups.at[t],
            dst_ref=arrived.at[e],
            send_sem=send2.at[t, core],
            recv_sem=recv2.at[e],
            device_id=(2 * z + core, 8 * k + t),
            device_id_type=MESH,
        )

    for d in range(8):
        t = (z - d) % 8
        if d > 0:
            shared[d - 1].wait_recv()
        for core in (0, 1):
            itself = (core == k) & (8 * k + t == e)

            @pl.when(jnp.logical_not(itself))
            def _():
                hand_over(t, core).start()

            @pl.when(itself)
            def _():
                arrived[e] = groups[t]

    for s in range(16):
        itself = (e == s) & (e // 8 == k)

        @pl.when(jnp.logical_not(itself))
        def _():
            pltpu.make_async_remote_copy(
                src_ref=groups.at[0],
                dst_ref=arrived.at[s],
                send_sem=send2.at[0, 0],
                recv_sem=recv2.at[s],
                device_id=sibling,
                device_id_type=MESH,
            ).wait_recv()

    out[...] = arrived[...]
    for t in range(8):
        for core in (0, 1):
            itself = (core == k) & (8 * k + t == e)

            @pl.when(jnp.logical_not(itself))
            def _():
                hand_over(t, core).wait_send()

    wires.drain()


def project(vals, w_o):
    vmem = pl.BlockSpec(memory_space=VMEM)
    width = HEADS_DEV * VD
    copies = GATHER_COPIES + 1 + 14
    return pl.pallas_call(
        project_kernel,
        out_shape=jax.ShapeDtypeStruct((16, GROUP, COLS), jnp.bfloat16),
        in_specs=[vmem, vmem],
        out_specs=vmem,
        scratch_shapes=[
            VMEM((16, GROUP, width), jnp.bfloat16),
            VMEM((16, GROUP, COLS), jnp.bfloat16),
            VMEM((8, GROUP, COLS), jnp.bfloat16),
            VMEM((8, GROUP, COLS), jnp.bfloat16),
            VMEM((7, GROUP, COLS), jnp.bfloat16),
            VMEM((8, GROUP, COLS), jnp.bfloat16),
            VMEM((16, GROUP, COLS), jnp.bfloat16),
            pltpu.SemaphoreType.DMA((copies,)),
            pltpu.SemaphoreType.DMA((copies,)),
            pltpu.SemaphoreType.DMA((8, 2)),
            pltpu.SemaphoreType.DMA((16,)),
        ],
        compiler_params=pltpu.CompilerParams(
            collective_id=2, has_side_effects=True, vmem_limit_bytes=LIMIT
        ),
    )(vals, w_o)


def experts_kernel(
    normed, shares, residual, gate, up, down, s_gate, s_up, s_down,
    out, rows, w_in, w_out, mid, rx_mid, parts,
    b1r, b1l, btr, btl, b2r, b2l, a_in, a1r, a1l, atr, atl, a2r, a2l,
    zsum, rx_z, final, send, recv, z_send, z_recv, f_send, f_recv, load,
):
    place = Place()
    z, k, a, b, c, e = place.z, place.k, place.a, place.b, place.c, place.e
    sibling = place.sibling()
    a_right, a_left = place.plane(a + 1, b), place.plane(a - 1, b)
    b_right, b_left = place.plane(a, b + 1), place.plane(a, b - 1)
    partners = [sibling, a_right, a_left, b_right, b_left]
    partners += [place.along_z(d) for d in range(1, 8)]
    greet(partners)
    wires = Wires(send, recv)
    half = pl.ds(k * HALF, HALF)
    mine = b * 4 + a
    rows[mine, :, 0:HALF] = normed[:, half]
    rows[mine, :, HALF:WIDE] = shares[...]
    loads = []
    for i, (src, dst) in enumerate(
        (
            (gate.at[0, half, :], w_in.at[:, pl.ds(0, FF)]),
            (up.at[0, half, :], w_in.at[:, pl.ds(FF, FF)]),
            (s_gate, w_in.at[:, pl.ds(2 * FF, FF)]),
            (s_up, w_in.at[:, pl.ds(3 * FF, FF)]),
            (down.at[0, :, half], w_out.at[pl.ds(0, FF), :]),
            (s_down, w_out.at[pl.ds(FF, FF), :]),
        )
    ):
        made = pltpu.make_async_copy(src, dst, load.at[i])
        made.start()
        loads.append(made)
    finish = plane_gather(place, wires, rows, HALF // 2)
    for made in loads:
        made.wait()
    finish()
    product = jnp.dot(
        rows[:, :, 0:HALF].reshape(256, HALF), w_in[...], preferred_element_type=jnp.float32
    )
    mid[...] = product.reshape(16, 16, 4 * FF)
    swap = wires.copy(mid, rx_mid, sibling)
    extra = rows[:, :, HALF:WIDE].reshape(256, EXT).astype(jnp.float32)
    lane = lax.broadcasted_iota(jnp.int32, (256, EXT), 1)
    share = jnp.sum(
        jnp.where((lane == e) | (lane == e + 16), extra, 0.0), axis=1, keepdims=True
    )
    swap.wait_recv()
    hidden = []
    for s in range(16):
        t = (s % 4) * 4 + s // 4
        own = mid[s]
        other = rx_mid[t]
        g0 = own[:, 0:FF] + other[:, 2 * FF : 3 * FF]
        u0 = own[:, FF : 2 * FF] + other[:, 3 * FF : 4 * FF]
        g1 = own[:, 2 * FF : 3 * FF] + other[:, 0:FF]
        u1 = own[:, 3 * FF : 4 * FF] + other[:, FF : 2 * FF]
        h0 = (jax.nn.silu(g0) * u0).astype(jnp.bfloat16)
        h1 = (jax.nn.silu(g1) * u1).astype(jnp.bfloat16)
        hidden.append(jnp.concatenate([h0, h1], axis=1))
    hidden = jnp.concatenate(hidden, axis=0)
    produced = jnp.dot(hidden, w_out[...], preferred_element_type=jnp.float32) * share
    parts[...] = produced.astype(jnp.bfloat16).reshape(16, 16, HALF)

    total = ring_sum(
        wires,
        b_right,
        b_left,
        lambda d: parts.at[pl.ds(((b + d) % 4) * 4, 4)],
        b1r, b1l, btr, btl, b2r, b2l, HALF // 2,
    )
    a_in[...] = total.astype(jnp.bfloat16)
    total = ring_sum(
        wires,
        a_right,
        a_left,
        lambda d: a_in.at[(a + d) % 4],
        a1r, a1l, atr, atl, a2r, a2l, HALF // 2,
    )
    for i in range(7):
        zsum[i] = total[:, i * PIECE : (i + 1) * PIECE].astype(jnp.bfloat16)

    def spread(d):
        t = (z + d) % 8
        return t < 7, pltpu.make_async_remote_copy(
            src_ref=zsum.at[t % 7],
            dst_ref=rx_z.at[d - 1],
            send_sem=z_send.at[d - 1],
            recv_sem=z_recv.at[d - 1],
            device_id=place.along_z(d),
            device_id_type=MESH,
        )

    for d in range(1, 8):
        used, made = spread(d)

        @pl.when(used)
        def _():
            made.start()

    def share_final(d):
        return pltpu.make_async_remote_copy(
            src_ref=final.at[k, z % 7],
            dst_ref=final.at[k, z % 7],
            send_sem=f_send.at[d - 1],
            recv_sem=f_recv.at[z],
            device_id=place.along_z(d),
            device_id_type=MESH,
        )

    @pl.when(z < 7)
    def _():
        at = z % 7
        mixed = residual[k * 7 + at] + zsum[at].astype(jnp.float32)
        for d in range(1, 8):
            spread(d)[1].wait_recv()
            mixed = mixed + rx_z[d - 1].astype(jnp.float32)
        final[k, at] = mixed.astype(jnp.bfloat16)
        for d in range(1, 8):
            share_final(d).start()

    passed = []
    for i in range(7):

        @pl.when(z != i)
        def _():
            pltpu.make_async_remote_copy(
                src_ref=final.at[k, i],
                dst_ref=final.at[k, i],
                send_sem=f_send.at[0],
                recv_sem=f_recv.at[i],
                device_id=sibling,
                device_id_type=MESH,
            ).wait_recv()

        passed.append(wires.copy(final.at[k, i], final.at[k, i], sibling))
    for made in passed:
        made.wait_recv()
    for j in range(2):
        for i in range(7):
            start = j * HALF + i * PIECE
            out[:, start : start + PIECE] = final[j, i]
    for d in range(1, 8):
        used, made = spread(d)

        @pl.when(used)
        def _():
            made.wait_send()

        @pl.when(z < 7)
        def _():
            share_final(d).wait_send()

    wires.drain()


def experts(normed, shares, residual, w_gate, w_up, w_down, s_gate, s_up, s_down):
    vmem = pl.BlockSpec(memory_space=VMEM)
    anywhere = pl.BlockSpec(memory_space=ANY)
    copies = GATHER_COPIES + 1 + 8 + 7
    bf16, f32 = jnp.bfloat16, jnp.float32
    half = HALF // 2
    return pl.pallas_call(
        experts_kernel,
        out_shape=jax.ShapeDtypeStruct((GROUP, D), bf16),
        in_specs=[vmem] * 3 + [anywhere] * 6,
        out_specs=vmem,
        scratch_shapes=[
            VMEM((16, GROUP, WIDE), bf16),
            VMEM((HALF, 4 * FF), bf16),
            VMEM((2 * FF, HALF), bf16),
            VMEM((16, GROUP, 4 * FF), f32),
            VMEM((16, GROUP, 4 * FF), f32),
            VMEM((16, GROUP, HALF), bf16),
            VMEM((4, GROUP, half), bf16),
            VMEM((4, GROUP, half), bf16),
            VMEM((4, GROUP, HALF), bf16),
            VMEM((4, GROUP, HALF), bf16),
            VMEM((4, GROUP, HALF), bf16),
            VMEM((4, GROUP, HALF), bf16),
            VMEM((4, GROUP, HALF), bf16),
            VMEM((GROUP, half), bf16),
            VMEM((GROUP, half), bf16),
            VMEM((GROUP, HALF), bf16),
            VMEM((GROUP, HALF), bf16),
            VMEM((GROUP, HALF), bf16),
            VMEM((GROUP, HALF), bf16),
            VMEM((7, GROUP, PIECE), bf16),
            VMEM((7, GROUP, PIECE), bf16),
            VMEM((2, 7, GROUP, PIECE), bf16),
            pltpu.SemaphoreType.DMA((copies,)),
            pltpu.SemaphoreType.DMA((copies,)),
            pltpu.SemaphoreType.DMA((7,)),
            pltpu.SemaphoreType.DMA((7,)),
            pltpu.SemaphoreType.DMA((7,)),
            pltpu.SemaphoreType.DMA((8,)),
            pltpu.SemaphoreType.DMA((6,)),
        ],
        compiler_params=pltpu.CompilerParams(
            collective_id=3, has_side_effects=True, vmem_limit_bytes=LIMIT
        ),
    )(normed, shares, residual, w_gate, w_up, w_down, s_gate, s_up, s_down)


def body(
    q_pref,
    kv_pref,
    dec_q,
    dec_kv,
    page_req,
    dec_len,
    w_uv,
    w_o,
    x_dec,
    norm_gain,
    router,
    routes,
    w_gate,
    w_up,
    w_down,
):
    keys, s_gate, s_up, s_down = gather_keys(kv_pref, w_gate, w_up, w_down)
    pages = keys.reshape(16 * TOK // PAGE, PAGE, LAT)
    head_vals = decode_attention(
        page_req, dec_len, jnp.swapaxes(dec_q, 0, 1), dec_kv, pages, w_uv
    )
    head_out = project(head_vals, w_o)
    head_out = jnp.swapaxes(head_out, 0, 1).reshape(GROUP, D)
    residual = x_dec.astype(jnp.float32) + head_out.astype(jnp.float32)
    normed = (
        residual
        * lax.rsqrt(jnp.mean(residual * residual, axis=-1, keepdims=True) + 1e-06)
        * norm_gain.astype(jnp.float32)
    ).astype(jnp.bfloat16)
    affinity = jax.nn.sigmoid(jnp.dot(normed, router, preferred_element_type=jnp.float32))
    chosen = routes[:, :, None] == jnp.arange(router.shape[1])[None, None, :]
    picked = jnp.sum(jnp.where(chosen, affinity[:, None, :], 0.0), axis=2)
    gate_share = 2.5 * picked / jnp.sum(picked, axis=1, keepdims=True)
    per_expert = jnp.sum(jnp.where(chosen, gate_share[:, :, None], 0.0), axis=1)
    high = per_expert.astype(jnp.bfloat16)
    low = (per_expert - high.astype(jnp.float32)).astype(jnp.bfloat16)
    shares = jnp.concatenate([high, low, jnp.zeros((GROUP, EXT - 32), jnp.bfloat16)], axis=1)
    pieces = jnp.swapaxes(residual.reshape(GROUP, 14, PIECE), 0, 1)
    decode_out = experts(
        normed, shares, pieces, w_gate, w_up, w_down, s_gate, s_up, s_down
    )
    pref_out = prefill(q_pref, keys.reshape(16 * TOK, LAT))
    return (pref_out, decode_out)


def solution(mesh):
    placed = (
        P("ctx", "exp", None),
        P("ctx", None),
        P("exp", "ctx", None),
        P("exp", None),
        P("exp", None),
        P("exp"),
        P("ctx", None, None),
        P("ctx", "exp"),
        P("exp", None),
        P(),
        P(),
        P("exp", None),
        P("exp", None, "ctx"),
        P("exp", None, "ctx"),
        P("exp", "ctx", None),
    )
    return jax.shard_map(
        body,
        mesh=mesh,
        in_specs=placed,
        out_specs=(P("ctx", "exp", None), P("exp", None)),
        check_vma=False,
    )
```

```python
import functools

import jax
import jax.numpy as jnp
from jax import lax
from jax.experimental import pallas as pl
from jax.experimental.pallas import tpu as pltpu
from jax.sharding import PartitionSpec as P

D = 7168
HALF = D // 2
KVL = 512
LAT = 576
HEADS_DEV = 8
VD = 128
FF = 128
TOK = 128
PAGE = 16
GROUP = 16
COLS = 448
EXT = 128
FAR = 1 << 20

qk_scale = 192.0 ** (-0.5)
neg_big = -1e30
MESH = pl.DeviceIdType.MESH
VMEM = pltpu.VMEM
ANY = pl.ANY
LIMIT = 60 * 1024 * 1024


class Place:
    def __init__(self):
        self.c = lax.axis_index("ctx")
        self.e = lax.axis_index("exp")
        self.z, self.k = self.c // 2, self.c % 2
        x, y = self.e // 4, self.e % 4
        self.a = x + self.k * (y - x)
        self.b = y + self.k * (x - y)

    def exp_of(self, a, b):
        return (a + self.k * (b - a)) * 4 + b + self.k * (a - b)

    def plane(self, a, b):
        return (self.c, self.exp_of(a % 4, b % 4))

    def sibling(self):
        return (self.c + 1 - 2 * self.k, self.e)

    def along_z(self, step):
        return (((self.z + step) % 8) * 2 + self.k, self.e)


def greet(devices):
    barrier = pltpu.get_barrier_semaphore()
    for device in devices:
        pl.semaphore_signal(barrier, inc=1, device_id=device, device_id_type=MESH)
    pl.semaphore_wait(barrier, len(devices))


class Wires:
    def __init__(self, send_sem, recv_sem):
        self.send_sem, self.recv_sem = send_sem, recv_sem
        self.count = 0
        self.open = []

    def copy(self, src, dst, device):
        i = self.count
        self.count += 1
        made = pltpu.make_async_remote_copy(
            src_ref=src,
            dst_ref=dst,
            send_sem=self.send_sem.at[i],
            recv_sem=self.recv_sem.at[i],
            device_id=device,
            device_id_type=MESH,
        )
        made.start()
        self.open.append(made)
        return made

    def drain(self):
        for made in self.open:
            made.wait_send()
        self.open = []


def arrive(copies):
    for made in copies:
        made.wait_recv()


def f32(value):
    return value.astype(jnp.float32)


def bf16(value):
    return value.astype(jnp.bfloat16)


Z_STEPS = (4, 3, -3, 2, -2, 1, -1)
PLANE_STEPS = (
    (2, 2), (2, 1), (2, 3), (1, 2), (3, 2), (1, 1), (1, 3), (3, 1), (3, 3),
    (2, 0), (0, 2), (1, 0), (3, 0), (0, 1), (0, 3),
)
RING_STEPS = (2, 1, 3)
CHUNKS = 2
COPIES = 7 + 1 + 3 + 17 + 15 + 15 + 1 + 7 + 7 + 15 + 1 + 15 + 1 + 6 * CHUNKS + 7 + 7 + 1


def layer_kernel(
    pages, lengths, kv_t, dec_q, dec_kv, x_dec, gain, router_t, routes,
    q_t, w_uv, w_o_t, gate, up, down,
    pref, out,
    keys, cache, v_q, v_uv, v_o, w_in, w_out, latent, vals, parts, blocks, rx_half, red, rx_z,
    spread, rows, sums, rx_sums, marks, mid, rx_mid, made_rows, rx_b, mid_b, rx_a,
    zsum, rx_z2, final, send, recv, load,
):
    place = Place()
    z, k, a, b, c, e = place.z, place.k, place.a, place.b, place.c, place.e
    sibling = place.sibling()
    half = pl.ds(k * HALF, HALF)
    other_half = pl.ds((1 - k) * HALF, HALF)
    loads = []
    for i, (src, dst) in enumerate(
        (
            (w_uv, v_uv),
            (w_o_t, v_o),
            (gate.at[0, half, :], w_in.at[:, pl.ds(0, FF)]),
            (up.at[0, half, :], w_in.at[:, pl.ds(FF, FF)]),
            (down.at[0, :, half], w_out.at[pl.ds(0, FF), :]),
            (q_t, v_q),
        )
    ):
        made = pltpu.make_async_copy(src, dst, load.at[i])
        made.start()
        loads.append(made)
    keys[k, z] = jnp.transpose(kv_t[...])

    source = [pages[0, i] // 8 for i in range(16)]
    rank = []
    for i in range(16):
        before = jnp.int32(0)
        for j in range(i):
            before = before + jnp.where(source[j] == source[i], 1, 0)
        rank.append(before)
    for j in range(2):
        wanted = jnp.int32(0)
        for i in range(16):
            wanted = jnp.where((source[i] == c) & (rank[i] == j), pages[0, i] % 8, wanted)
        page = keys[k, z, 0:PAGE, :]
        for i in range(1, 8):
            page = jnp.where(wanted == i, keys[k, z, i * PAGE : (i + 1) * PAGE, :], page)
        cache[k, z, j * PAGE : (j + 1) * PAGE, :] = page

    greet(
        [sibling]
        + [place.along_z(d) for d in Z_STEPS]
        + [place.plane(a + i, b + j) for i, j in PLANE_STEPS]
    )
    wires = Wires(send, recv)
    mine = cache.at[k, z]
    page_copies = [wires.copy(mine, mine, place.along_z(d)) for d in Z_STEPS]
    swaps = [
        wires.copy(gate.at[0, other_half, :], w_in.at[:, pl.ds(2 * FF, FF)], sibling),
        wires.copy(up.at[0, other_half, :], w_in.at[:, pl.ds(3 * FF, FF)], sibling),
        wires.copy(down.at[0, :, other_half], w_out.at[pl.ds(FF, FF), :], sibling),
    ]

    count = HEADS_DEV * GROUP
    queries = dec_q[...].reshape(count, LAT)
    own = jnp.broadcast_to(f32(dec_kv[...])[:, None, :], (GROUP, HEADS_DEV, LAT))
    own = own.reshape(count, LAT)
    own_score = jnp.sum(f32(queries) * own, axis=1, keepdims=True)
    row = lax.broadcasted_iota(jnp.int32, (count, 1), 0) // HEADS_DEV
    limit = jnp.zeros((count, 1), jnp.int32)
    for i in range(GROUP):
        limit = jnp.where(row == i, lengths[i], limit)
    lane = lax.broadcasted_iota(jnp.int32, (1, 256), 1)
    allowed = []
    for core in (k, 1 - k):
        position = jnp.full((1, 256), FAR, jnp.int32)
        for i in range(16):
            here = ((lane // 32) * 2 + core == source[i]) & ((lane // PAGE) % 2 == rank[i])
            position = jnp.where(here, i * PAGE + lane % PAGE, position)
        allowed.append(position < limit)
    arrive(page_copies)
    to_sibling = wires.copy(cache.at[k], cache.at[k], sibling)
    block = keys.at[k, z]
    to_r = wires.copy(block, block, place.along_z(1))
    to_l = wires.copy(block, block, place.along_z(-1))
    key_copies = [wires.copy(block, block, sibling)]

    def ring_hop(hop, to_r, to_l):
        to_r.wait_recv()
        to_l.wait_recv()
        if hop == 4:
            ref = keys.at[k, (z + 4) % 8]
            key_copies.append(wires.copy(ref, ref, sibling))
            return None, None
        first, second = keys.at[k, (z - hop) % 8], keys.at[k, (z + hop) % 8]
        right, left = first, second
        if hop == 3:
            right = keys.at[k, (z - hop) % 8, pl.ds(0, TOK // 2), :]
            left = keys.at[k, (z + hop) % 8, pl.ds(TOK // 2, TOK // 2), :]
        to_r = wires.copy(right, right, place.along_z(1))
        to_l = wires.copy(left, left, place.along_z(-1))
        key_copies.append(wires.copy(first, first, sibling))
        key_copies.append(wires.copy(second, second, sibling))
        return to_r, to_l

    scores = []
    for i, core in enumerate((k, 1 - k)):
        if i == 1:
            to_sibling.wait_recv()
        cached = cache[core].reshape(256, LAT)
        score = lax.dot_general(
            queries, cached, (((1,), (1,)), ((), ())), preferred_element_type=jnp.float32
        )
        scores.append(jnp.where(allowed[i], score, neg_big))
    top = jnp.maximum(jnp.max(scores[0], axis=1, keepdims=True), own_score)
    top = jnp.maximum(jnp.max(scores[1], axis=1, keepdims=True), top)
    own_weight = jnp.exp((own_score - top) * qk_scale)
    total = own_weight
    mixed = f32(bf16(own_weight)) * own[:, :KVL]
    for i, core in enumerate((k, 1 - k)):
        weights = jnp.where(allowed[i], jnp.exp((scores[i] - top) * qk_scale), 0.0)
        total = total + jnp.sum(weights, axis=1, keepdims=True)
        cached = cache[core].reshape(256, LAT)
        mixed = mixed + jnp.dot(
            bf16(weights), cached[:, :KVL], preferred_element_type=jnp.float32
        )
    mixed = mixed / total
    for i in range(KVL // 128):
        latent[i] = mixed[:, i * 128 : (i + 1) * 128]
    loads[0].wait()
    for h in range(HEADS_DEV):
        every = pl.ds(h, GROUP, stride=HEADS_DEV)
        part = jnp.concatenate([latent[i, every, :] for i in range(KVL // 128)], axis=1)
        part = jnp.dot(bf16(part), v_uv[h], preferred_element_type=jnp.float32)
        vals[e, :, h * VD : (h + 1) * VD] = bf16(part)

    near = [place.plane(a + i, b + j) for i, j in PLANE_STEPS]
    copies = [wires.copy(vals.at[e], vals.at[e], device) for device in near]
    to_r, to_l = ring_hop(1, to_r, to_l)
    loads[1].wait()
    arrive(copies)
    product = lax.dot_general(
        vals[...].reshape(256, HEADS_DEV * VD),
        v_o[...],
        (((1,), (1,)), ((), ())),
        preferred_element_type=jnp.float32,
    )
    parts[...] = bf16(product).reshape(16, GROUP, COLS)
    copies = [wires.copy(parts.at[device[1]], blocks.at[e], device) for device in near]
    blocks[e] = parts[e]
    to_r, to_l = ring_hop(2, to_r, to_l)
    arrive(copies)
    to_sibling = wires.copy(blocks.at[pl.ds((1 - k) * 8, 8)], rx_half, sibling)
    to_sibling.wait_recv()
    red[...] = bf16(f32(blocks[pl.ds(k * 8, 8)]) + f32(rx_half[...]))

    def sum_z(ref, rx):
        copies = []
        for i, d in enumerate(Z_STEPS):
            copies.append(wires.copy(ref.at[(z + d) % 8], rx.at[i], place.along_z(d)))
        total = f32(ref[z])
        for i in range(7):
            copies[i].wait_recv()
            total = total + f32(rx[i])
        return total

    pair = pl.ds((k * 4 + z // 2) * 2 * COLS, 2 * COLS)
    odd = z % 2 == 1
    x_pair, gain_pair = f32(x_dec[:, pair]), f32(gain[:, pair])
    x_own = jnp.where(odd, x_pair[:, COLS:], x_pair[:, :COLS])
    gain_own = jnp.where(odd, gain_pair[:, COLS:], gain_pair[:, :COLS])
    residual = x_own + sum_z(red, rx_z)
    spread[z] = bf16(residual * gain_own)
    copies = [wires.copy(spread.at[z], spread.at[z], place.along_z(d)) for d in Z_STEPS]
    arrive(copies)
    slot = b * 4 + a
    for i in range(8):
        rows[slot, :, i * COLS : (i + 1) * COLS] = spread[i]

    ref = rows.at[slot]
    along_a = [wires.copy(ref, ref, place.plane(a + d, b)) for d in RING_STEPS]
    along_b = [wires.copy(ref, ref, place.plane(a, b + d)) for d in RING_STEPS]
    scaled = rows[slot]
    logits = lax.dot_general(
        scaled, router_t[:, half], (((1,), (1,)), ((), ())), preferred_element_type=jnp.float32
    )
    gain_half = f32(gain[:, half])
    squares = f32(scaled) / gain_half
    squares = jnp.sum(squares * squares, axis=1, keepdims=True)
    lane = lax.broadcasted_iota(jnp.int32, (GROUP, EXT), 1)
    sums[:, 0:16] = logits
    sums[:, 16:EXT] = jnp.broadcast_to(squares, (GROUP, EXT - 16))
    to_sibling = wires.copy(sums, rx_sums, sibling)
    for i, d in zip((1, 2, 0), (1, 3, 2)):
        along_a[i].wait_recv()
        ref = rows.at[b * 4 + (a - d) % 4]
        along_b += [wires.copy(ref, ref, place.plane(a, b + j)) for j in RING_STEPS]
        if i == 1:
            to_sibling.wait_recv()
            both = sums[...] + rx_sums[...]
            scale = lax.rsqrt(both[:, 16:17] / D + 1e-06)
            affinity = jax.nn.sigmoid(both * scale)
            chosen = lane == routes[:, 0:1]
            for t in range(1, routes.shape[1]):
                chosen = chosen | (lane == routes[:, t : t + 1])
            picked = jnp.where(chosen, affinity, 0.0)
            share = 2.5 * picked / jnp.sum(picked, axis=1, keepdims=True)
            marks[slot] = jnp.where(lane == 16, scale, share)
            mark_copies = [wires.copy(marks.at[slot], marks.at[slot], device) for device in near]
    to_r, to_l = ring_hop(3, to_r, to_l)

    key_at = lax.broadcasted_iota(jnp.int32, (1, 16 * TOK), 1)
    key_at = (((key_at // TOK) % 8) * 2 + key_at // (8 * TOK)) * TOK + key_at % TOK

    def prefill_tile(i):
        queries = jnp.concatenate(
            [jnp.transpose(v_q[2 * i]), jnp.transpose(v_q[2 * i + 1])], axis=0
        )
        all_keys = keys[...].reshape(16 * TOK, LAT)
        scores = lax.dot_general(
            queries, all_keys, (((1,), (1,)), ((), ())), preferred_element_type=jnp.float32
        )
        token = c * TOK + lax.broadcasted_iota(jnp.int32, (2 * TOK, 1), 0) % TOK
        scores = jnp.where(key_at <= token, scores, neg_big)
        top = jnp.max(scores, axis=1, keepdims=True)
        weights = jnp.exp((scores - top) * qk_scale)
        total = jnp.sum(weights, axis=1, keepdims=True)
        mixed = jnp.dot(
            bf16(weights), all_keys[:, :KVL], preferred_element_type=jnp.float32
        )
        pref[2 * i : 2 * i + 2] = bf16(mixed / total).reshape(2, TOK, KVL)

    arrive(along_b)
    for made in loads[2:]:
        made.wait()
    arrive(swaps)

    product = jnp.dot(
        rows[...].reshape(256, HALF), w_in[...], preferred_element_type=jnp.float32
    )
    mid[...] = product.reshape(16, GROUP, 4 * FF)
    to_sibling = wires.copy(mid, rx_mid, sibling)
    arrive(mark_copies)
    mark = marks[...].reshape(256, EXT)
    lane = lax.broadcasted_iota(jnp.int32, (256, EXT), 1)
    share = jnp.sum(jnp.where(lane == e, mark, 0.0), axis=1, keepdims=True)
    scale = mark[:, 16:17]
    ring_hop(4, to_r, to_l)
    to_sibling.wait_recv()
    hidden = []
    for s in range(16):
        own, other = mid[s], rx_mid[(s % 4) * 4 + s // 4]
        at = scale[s * GROUP : (s + 1) * GROUP]
        g0 = (own[:, 0:FF] + other[:, 2 * FF : 3 * FF]) * at
        u0 = (own[:, FF : 2 * FF] + other[:, 3 * FF : 4 * FF]) * at
        g1 = (own[:, 2 * FF : 3 * FF] + other[:, 0:FF]) * at
        u1 = (own[:, 3 * FF : 4 * FF] + other[:, FF : 2 * FF]) * at
        h0 = bf16(jax.nn.silu(g0) * u0)
        h1 = bf16(jax.nn.silu(g1) * u1)
        hidden.append(jnp.concatenate([h0, h1], axis=1))
    hidden = jnp.concatenate(hidden, axis=0)
    produced = jnp.dot(hidden, w_out[...], preferred_element_type=jnp.float32) * share
    made_rows[...] = bf16(produced).reshape(16, GROUP, HALF)

    width = HALF // CHUNKS
    first = []
    for i in range(CHUNKS):
        cols = pl.ds(i * width, width)
        for j, d in enumerate(RING_STEPS):
            src = made_rows.at[pl.ds(((b + d) % 4) * 4, 4), :, cols]
            first.append(wires.copy(src, rx_b.at[j, :, :, cols], place.plane(a, b + d)))
    arrive(key_copies)
    for i in range(3):
        prefill_tile(i)
    second = []
    for i in range(CHUNKS):
        cols = slice(i * width, (i + 1) * width)
        arrive(first[3 * i : 3 * i + 3])
        total = f32(made_rows[pl.ds(b * 4, 4), :, cols])
        for j in range(3):
            total = total + f32(rx_b[j, :, :, cols])
        mid_b[:, :, cols] = bf16(total)
        cols = pl.ds(i * width, width)
        for j, d in enumerate(RING_STEPS):
            src = mid_b.at[(a + d) % 4, :, cols]
            second.append(wires.copy(src, rx_a.at[j, :, cols], place.plane(a + d, b)))
    prefill_tile(3)
    arrive(second)
    total = f32(mid_b[a])
    for j in range(3):
        total = total + f32(rx_a[j])
    for i in range(8):
        zsum[i] = bf16(total[:, i * COLS : (i + 1) * COLS])
    final[k, z] = bf16(residual + sum_z(zsum, rx_z2))
    ref = final.at[k, z]
    arrive([wires.copy(ref, ref, place.along_z(d)) for d in Z_STEPS])
    to_sibling = wires.copy(final.at[k], final.at[k], sibling)
    to_sibling.wait_recv()
    for i in range(16):
        out[:, i * COLS : (i + 1) * COLS] = final[i // 8, i % 8]
    wires.drain()


def layer(*args):
    vmem, smem = pl.BlockSpec(memory_space=VMEM), pl.BlockSpec(memory_space=pltpu.SMEM)
    anywhere = pl.BlockSpec(memory_space=ANY)
    half, full = jnp.bfloat16, jnp.float32
    scratch = [
        ((2, 8, TOK, LAT), half),
        ((2, 8, 2 * PAGE, LAT), half),
        ((HEADS_DEV, LAT, TOK), half),
        ((HEADS_DEV, KVL, VD), half),
        ((COLS, HEADS_DEV * VD), half),
        ((HALF, 4 * FF), half),
        ((2 * FF, HALF), half),
        ((KVL // 128, GROUP * HEADS_DEV, 128), full),
        ((16, GROUP, HEADS_DEV * VD), half),
        ((16, GROUP, COLS), half),
        ((16, GROUP, COLS), half),
        ((8, GROUP, COLS), half),
        ((8, GROUP, COLS), half),
        ((7, GROUP, COLS), half),
        ((8, GROUP, COLS), half),
        ((16, GROUP, HALF), half),
        ((GROUP, EXT), full),
        ((GROUP, EXT), full),
        ((16, GROUP, EXT), full),
        ((16, GROUP, 4 * FF), full),
        ((16, GROUP, 4 * FF), full),
        ((16, GROUP, HALF), half),
        ((3, 4, GROUP, HALF), half),
        ((4, GROUP, HALF), half),
        ((3, GROUP, HALF), half),
        ((8, GROUP, COLS), half),
        ((7, GROUP, COLS), half),
        ((2, 8, GROUP, COLS), half),
    ]
    return pl.pallas_call(
        layer_kernel,
        out_shape=(
            jax.ShapeDtypeStruct((HEADS_DEV, TOK, KVL), half),
            jax.ShapeDtypeStruct((GROUP, D), half),
        ),
        in_specs=[smem] * 2 + [vmem] * 7 + [anywhere] * 6,
        out_specs=[vmem] * 2,
        scratch_shapes=[VMEM(shape, dtype) for shape, dtype in scratch]
        + [
            pltpu.SemaphoreType.DMA((COPIES,)),
            pltpu.SemaphoreType.DMA((COPIES,)),
            pltpu.SemaphoreType.DMA((6,)),
        ],
        compiler_params=pltpu.CompilerParams(
            collective_id=1, has_side_effects=True, vmem_limit_bytes=LIMIT
        ),
    )(*args)


def body(
    q_pref,
    kv_pref,
    dec_q,
    dec_kv,
    page_req,
    dec_len,
    w_uv,
    w_o,
    x_dec,
    norm_gain,
    router,
    routes,
    w_gate,
    w_up,
    w_down,
):
    pref, decode_out = layer(
        page_req,
        dec_len,
        kv_pref.T,
        dec_q,
        dec_kv,
        x_dec,
        norm_gain.reshape(1, D),
        router.T,
        routes,
        jnp.transpose(q_pref, (1, 2, 0)),
        w_uv,
        w_o.T,
        w_gate,
        w_up,
        w_down,
    )
    return (jnp.swapaxes(pref, 0, 1), decode_out)


def solution(mesh):
    placed = (
        P("ctx", "exp", None),
        P("ctx", None),
        P("exp", "ctx", None),
        P("exp", None),
        P("exp", None),
        P("exp"),
        P("ctx", None, None),
        P("ctx", "exp"),
        P("exp", None),
        P(),
        P(),
        P("exp", None),
        P("exp", None, "ctx"),
        P("exp", None, "ctx"),
        P("exp", "ctx", None),
    )
    return jax.shard_map(
        body,
        mesh=mesh,
        in_specs=placed,
        out_specs=(P("ctx", "exp", None), P("exp", None)),
        check_vma=False,
    )
```

```python
import functools

import jax
import jax.numpy as jnp
from jax import lax
from jax.experimental import pallas as pl
from jax.experimental.pallas import tpu as pltpu
from jax.sharding import PartitionSpec as P

D = 7168
HALF = D // 2
KVL = 512
LAT = 576
HEADS_DEV = 8
VD = 128
FF = 128
TOK = 128
PAGE = 16
GROUP = 16
COLS = 448
EXT = 128
FAR = 1 << 20

qk_scale = 192.0 ** (-0.5)
neg_big = -1e30
MESH = pl.DeviceIdType.MESH
VMEM = pltpu.VMEM
ANY = pl.ANY
LIMIT = 60 * 1024 * 1024


class Place:
    def __init__(self):
        self.c = lax.axis_index("ctx")
        self.e = lax.axis_index("exp")
        self.z, self.k = self.c // 2, self.c % 2
        x, y = self.e // 4, self.e % 4
        self.a = x + self.k * (y - x)
        self.b = y + self.k * (x - y)

    def exp_of(self, a, b):
        return (a + self.k * (b - a)) * 4 + b + self.k * (a - b)

    def plane(self, a, b):
        return (self.c, self.exp_of(a % 4, b % 4))

    def sibling(self):
        return (self.c + 1 - 2 * self.k, self.e)

    def along_z(self, step):
        return (((self.z + step) % 8) * 2 + self.k, self.e)


def greet(devices):
    barrier = pltpu.get_barrier_semaphore()
    for device in devices:
        pl.semaphore_signal(barrier, inc=1, device_id=device, device_id_type=MESH)
    return lambda: pl.semaphore_wait(barrier, len(devices))


class Wires:
    def __init__(self, send_sem, recv_sem):
        self.send_sem, self.recv_sem = send_sem, recv_sem
        self.count = 0
        self.open = []

    def copy(self, src, dst, device):
        i = self.count
        self.count += 1
        made = pltpu.make_async_remote_copy(
            src_ref=src,
            dst_ref=dst,
            send_sem=self.send_sem.at[i],
            recv_sem=self.recv_sem.at[i],
            device_id=device,
            device_id_type=MESH,
        )
        made.start()
        self.open.append(made)
        return made

    def drain(self):
        for made in self.open:
            made.wait_send()
        self.open = []


def arrive(copies):
    for made in copies:
        made.wait_recv()


def f32(value):
    return value.astype(jnp.float32)


def bf16(value):
    return value.astype(jnp.bfloat16)


Z_STEPS = (4, 3, -3, 2, -2, 1, -1)
PLANE_STEPS = (
    (2, 2), (2, 1), (2, 3), (1, 2), (3, 2), (1, 1), (1, 3), (3, 1), (3, 3),
    (2, 0), (0, 2), (1, 0), (3, 0), (0, 1), (0, 3),
)
RING_STEPS = (2, 1, 3)
PLACES = (0, 1, -1, -2, 2, -3, 3, 4)
PARTS = ((4, 2), (0, 4))
SUM_PARTS = ((0, 4), (4, 2))
COPIES = 7 + 1 + 17 + 17 + 15 + 15 + 1 + 7 + 12 + 30 + 8 + 1 + 15 + 1 + 8 + 12 + 5 + 7 + 1
LOADS = HEADS_DEV + 5 + 16 + 1 + 1


def layer_kernel(
    pages, lengths, kv_t, dec_q, dec_kv,
    x_dec_in, gain_in, router_in, routes_in, q_t, w_uv, w_o_t, gate, up, down,
    pref, out,
    x_dec, gain_rows, gain, router_t, routes, keys, keys_t, cache, v_q, v_uv, v_o, w_in, w_out, latent, vals, parts, blocks, rx_half, red, rx_z,
    rows, sums, rx_sums, marks, by_token, pref_rows, scores_at, weights_at, totals, mid, rx_mid, made_rows, rx_pre, rx_b, mid_b, rx_a,
    zsum, rx_z2, final, send, recv, load,
):
    place = Place()
    z, k, a, b, c, e = place.z, place.k, place.a, place.b, place.c, place.e
    sibling = place.sibling()
    half = pl.ds(k * HALF, HALF)
    other_half = pl.ds((1 - k) * HALF, HALF)
    def block_copies(side, at):
        pairs = []
        for p, d in enumerate(PLACES):
            block = pl.ds((side * 8 + (z + d) % 8) * COLS, COLS)
            pairs.append((gate.at[0, block, :], w_in.at[p, :, pl.ds(at * FF, FF)]))
            pairs.append((up.at[0, block, :], w_in.at[p, :, pl.ds((at + 1) * FF, FF)]))
        return pairs

    enter = greet(
        [sibling]
        + [place.along_z(d) for d in Z_STEPS]
        + [place.plane(a + i, b + j) for i, j in PLANE_STEPS]
    )
    loads = []
    for i, (src, dst) in enumerate(
        [(w_uv.at[h], v_uv.at[:, pl.ds(h * VD, VD)]) for h in range(HEADS_DEV)]
        + [
            (w_o_t, v_o),
            (x_dec_in, x_dec),
            (gain_in, gain_rows),
            (router_in, router_t),
            (routes_in, routes),
        ]
        + block_copies(k, 0)
        + [(down.at[0, :, half], w_out.at[pl.ds(0, FF), :]), (q_t, v_q)]
    ):
        made = pltpu.make_async_copy(src, dst, load.at[i])
        made.start()
        loads.append(made)
    keys[k, z] = jnp.transpose(kv_t[...])

    source = [pages[0, i] // 8 for i in range(16)]
    rank = []
    for i in range(16):
        before = jnp.int32(0)
        for j in range(i):
            before = before + jnp.where(source[j] == source[i], 1, 0)
        rank.append(before)
    for j in range(2):
        wanted = jnp.int32(0)
        for i in range(16):
            wanted = jnp.where((source[i] == c) & (rank[i] == j), pages[0, i] % 8, wanted)
        page = keys[k, z, 0:PAGE, :]
        for i in range(1, 8):
            page = jnp.where(wanted == i, keys[k, z, i * PAGE : (i + 1) * PAGE, :], page)
        cache[k, z, j * PAGE : (j + 1) * PAGE, :] = page

    enter()
    wires = Wires(send, recv)
    mine = cache.at[k, z]
    page_copies = [wires.copy(mine, mine, place.along_z(d)) for d in Z_STEPS]
    swaps = [wires.copy(src, dst, sibling) for src, dst in block_copies(1 - k, 2)]
    swaps.append(wires.copy(down.at[0, :, other_half], w_out.at[pl.ds(FF, FF), :], sibling))

    count = HEADS_DEV * GROUP
    queries = dec_q[...].reshape(count, LAT)
    own = jnp.broadcast_to(f32(dec_kv[...])[:, None, :], (GROUP, HEADS_DEV, LAT))
    own = own.reshape(count, LAT)
    own_score = jnp.sum(f32(queries) * own, axis=1, keepdims=True)
    row = lax.broadcasted_iota(jnp.int32, (count, 1), 0) // HEADS_DEV
    limit = jnp.zeros((count, 1), jnp.int32)
    for i in range(GROUP):
        limit = jnp.where(row == i, lengths[i], limit)
    lane = lax.broadcasted_iota(jnp.int32, (1, 256), 1)
    allowed = []
    for core in (k, 1 - k):
        position = jnp.full((1, 256), FAR, jnp.int32)
        for i in range(16):
            here = ((lane // 32) * 2 + core == source[i]) & ((lane // PAGE) % 2 == rank[i])
            position = jnp.where(here, i * PAGE + lane % PAGE, position)
        allowed.append(position < limit)
    arrive(page_copies)
    to_sibling = wires.copy(cache.at[k], cache.at[k], sibling)
    block = keys.at[k, z]
    to_r = wires.copy(block, block, place.along_z(1))
    to_l = wires.copy(block, block, place.along_z(-1))
    key_copies = [wires.copy(block, block, sibling)]

    def ring_hop(hop, to_r, to_l):
        to_r.wait_recv()
        to_l.wait_recv()
        if hop == 4:
            ref = keys.at[k, (z + 4) % 8]
            key_copies.append(wires.copy(ref, ref, sibling))
            return None, None
        first, second = keys.at[k, (z - hop) % 8], keys.at[k, (z + hop) % 8]
        right, left = first, second
        if hop == 3:
            right = keys.at[k, (z - hop) % 8, pl.ds(0, TOK // 2), :]
            left = keys.at[k, (z + hop) % 8, pl.ds(TOK // 2, TOK // 2), :]
        to_r = wires.copy(right, right, place.along_z(1))
        to_l = wires.copy(left, left, place.along_z(-1))
        key_copies.append(wires.copy(first, first, sibling))
        key_copies.append(wires.copy(second, second, sibling))
        return to_r, to_l

    scores = []
    for i, core in enumerate((k, 1 - k)):
        if i == 1:
            to_sibling.wait_recv()
        cached = cache[core].reshape(256, LAT)
        score = lax.dot_general(
            queries, cached, (((1,), (1,)), ((), ())), preferred_element_type=jnp.float32
        )
        scores.append(jnp.where(allowed[i], score, neg_big))
    top = jnp.maximum(jnp.max(scores[0], axis=1, keepdims=True), own_score)
    top = jnp.maximum(jnp.max(scores[1], axis=1, keepdims=True), top)
    own_weight = jnp.exp((own_score - top) * qk_scale)
    total = own_weight
    mixed = f32(bf16(own_weight)) * own[:, :KVL]
    for i, core in enumerate((k, 1 - k)):
        weights = jnp.where(allowed[i], jnp.exp((scores[i] - top) * qk_scale), 0.0)
        total = total + jnp.sum(weights, axis=1, keepdims=True)
        cached = cache[core].reshape(256, LAT)
        mixed = mixed + jnp.dot(
            bf16(weights), cached[:, :KVL], preferred_element_type=jnp.float32
        )
    for made in loads[:HEADS_DEV]:
        made.wait()
    product = jnp.dot(bf16(mixed / total), v_uv[...], preferred_element_type=jnp.float32)
    for h in range(HEADS_DEV):
        latent[h] = product[:, h * VD : (h + 1) * VD]
        part = latent[h, pl.ds(h, GROUP, stride=HEADS_DEV), :]
        vals[e, :, h * VD : (h + 1) * VD] = bf16(part)

    near = [place.plane(a + i, b + j) for i, j in PLANE_STEPS]
    copies = [wires.copy(vals.at[e], vals.at[e], device) for device in near]
    to_r, to_l = ring_hop(1, to_r, to_l)
    for made in loads[HEADS_DEV : HEADS_DEV + 5]:
        made.wait()
    for i in range(D // 128):
        gain[:, i * 128 : (i + 1) * 128] = f32(gain_rows[i : i + 1, :])
    arrive(copies)
    product = lax.dot_general(
        vals[...].reshape(256, HEADS_DEV * VD),
        v_o[...],
        (((1,), (1,)), ((), ())),
        preferred_element_type=jnp.float32,
    )
    parts[...] = bf16(product).reshape(16, GROUP, COLS)
    copies = [wires.copy(parts.at[device[1]], blocks.at[e], device) for device in near]
    blocks[e] = parts[e]
    to_r, to_l = ring_hop(2, to_r, to_l)
    arrive(copies)
    to_sibling = wires.copy(blocks.at[pl.ds((1 - k) * 8, 8)], rx_half, sibling)
    to_sibling.wait_recv()
    red[...] = bf16(f32(blocks[pl.ds(k * 8, 8)]) + f32(rx_half[...]))

    def sum_z(ref, rx, meanwhile):
        copies = []
        for i, d in enumerate(Z_STEPS):
            copies.append(wires.copy(ref.at[(z + d) % 8], rx.at[i], place.along_z(d)))
        total = f32(ref[z])
        meanwhile()
        for i in range(7):
            copies[i].wait_recv()
            total = total + f32(rx[i])
        return total

    pair = pl.ds((k * 4 + z // 2) * 2 * COLS, 2 * COLS)
    odd = z % 2 == 1
    x_pair, gain_pair, router_pair = f32(x_dec[:, pair]), gain[:, pair], f32(router_t[:, pair])
    x_own = jnp.where(odd, x_pair[:, COLS:], x_pair[:, :COLS])
    gain_own = jnp.where(odd, gain_pair[:, COLS:], gain_pair[:, :COLS])
    router_own = jnp.where(odd, router_pair[:, COLS:], router_pair[:, :COLS])
    ring = []
    residual = x_own + sum_z(red, rx_z, lambda: ring.extend(ring_hop(3, to_r, to_l)))
    scaled = bf16(residual * gain_own)
    slot = b * 4 + a
    rows[0, slot] = scaled
    spread = {}
    for p in (5, 4, 3, 1, 2):
        spread[p] = wires.copy(rows.at[0, slot], rows.at[p, slot], place.along_z(-PLACES[p]))

    ring_hop(4, *ring)

    lane = lax.broadcasted_iota(jnp.int32, (GROUP, EXT), 1)
    sums[z, :, 0:16] = lax.dot_general(
        scaled, bf16(router_own), (((1,), (1,)), ((), ())), preferred_element_type=jnp.float32
    )
    squares = jnp.sum(residual * residual, axis=1, keepdims=True)
    sums[z, :, 16:EXT] = jnp.broadcast_to(squares, (GROUP, EXT - 16))

    along_a, along_b = [], []

    def send_part(part):
        first, size = PARTS[part]
        for p in range(first, first + size):
            if p > 0:
                spread[p].wait_recv()
        ref = rows.at[pl.ds(first, size), slot]
        along_a.append([wires.copy(ref, ref, place.plane(a + d, b)) for d in RING_STEPS])
        along_b.append([wires.copy(ref, ref, place.plane(a, b + d)) for d in RING_STEPS])

    def pass_part(part):
        first, size = PARTS[part]
        for i, d in zip((1, 2, 0), (1, 3, 2)):
            along_a[part][i].wait_recv()
            ref = rows.at[pl.ds(first, size), b * 4 + (a - d) % 4]
            along_b[part] += [wires.copy(ref, ref, place.plane(a, b + j)) for j in RING_STEPS]

    passed = []

    def pass_z(j):
        group = pl.ds(((b + j) % 4) * 4, 4)
        for p, q, d in ((4, 6, -1), (5, 7, 1)):
            passed.append(wires.copy(rows.at[p, group], rows.at[q, group], place.along_z(d)))

    def pass_z_from(step):
        arrive(along_b[0][RING_STEPS.index(step) :: 3])
        pass_z(-step)

    send_part(0)
    send_part(1)
    sum_copies = [wires.copy(sums.at[z], sums.at[z], place.along_z(d)) for d in Z_STEPS]
    arrive(key_copies)
    for i in range(16):
        block = keys[i // 8, i % 8, :, 0:KVL]
        keys_t[:, i * TOK : (i + 1) * TOK] = jnp.transpose(block)
    loads[-1].wait()
    pass_part(0)
    pass_z(0)
    pass_part(1)
    arrive(sum_copies)
    total = sums[0]
    for i in range(1, 8):
        total = total + sums[i]
    rx_sums[k] = total
    to_sibling = wires.copy(rx_sums.at[k], rx_sums.at[k], sibling)
    pass_z_from(1)
    pass_z_from(3)
    to_sibling.wait_recv()
    both = rx_sums[0] + rx_sums[1]
    scale = lax.rsqrt(both[:, 16:17] / D + 1e-06)
    affinity = jax.nn.sigmoid(both * scale)
    itself = lax.broadcasted_iota(jnp.int32, (GROUP, GROUP), 0) == lax.broadcasted_iota(
        jnp.int32, (GROUP, GROUP), 1
    )
    chosen = lane < 0
    for t in range(routes.shape[0]):
        named = jnp.sum(jnp.where(itself, routes[t : t + 1, :], 0), axis=1, keepdims=True)
        chosen = chosen | (lane == named)
    picked = jnp.where(chosen, affinity, 0.0)
    share = 2.5 * picked / jnp.sum(picked, axis=1, keepdims=True)
    mark = jnp.where(lane == 16, scale, share)
    marks[slot] = jnp.where(lane[0:8] < 32, mark[0:8], pltpu.roll(mark[8:16], 32, 1))
    mark_copies = [wires.copy(marks.at[slot], marks.at[slot], device) for device in near]
    pass_z_from(2)
    def score_tile(i):
        queries = jnp.concatenate([v_q[2 * i], v_q[2 * i + 1]], axis=1)
        scores_at[i] = jnp.dot(
            keys[...].reshape(16 * TOK, LAT), queries, preferred_element_type=jnp.float32
        )

    def weigh_tile(i):
        shape = (TOK, 2 * TOK)
        ahead = lax.broadcasted_iota(jnp.int32, shape, 0)
        ahead = ahead - lax.broadcasted_iota(jnp.int32, shape, 1) % TOK

        def block(n):
            behind = (c - (n % 8) * 2 - n // 8) * TOK
            return jnp.where(ahead <= behind, scores_at[i, n * TOK : (n + 1) * TOK], neg_big)

        top = block(0)
        for n in range(1, 16):
            top = jnp.maximum(top, block(n))
        top = jnp.max(top, axis=0, keepdims=True)
        total = 0.0
        for n in range(16):
            weights = jnp.exp((block(n) - top) * qk_scale)
            total = total + weights
            weights_at[i, n * TOK : (n + 1) * TOK] = bf16(weights)
        totals[i : i + 1] = jnp.sum(total, axis=0, keepdims=True)

    def mix_tile(i):
        mixed = jnp.dot(keys_t[...], weights_at[i], preferred_element_type=jnp.float32)
        mixed = mixed / totals[i : i + 1]
        for j in range(2):
            head = jnp.transpose(mixed[:, j * TOK : (j + 1) * TOK])
            every = pl.ds(2 * i + j, TOK, stride=HEADS_DEV)
            for t in range(KVL // 128):
                by_token[t, every, :] = head[:, t * 128 : (t + 1) * 128]

    score_tile(0)
    score_tile(1)
    arrive(along_b[1])
    for made in loads[HEADS_DEV + 5 : -1]:
        made.wait()
    arrive(swaps)

    def product_of(places):
        total = 0.0
        for p in places:
            block = rows[p].reshape(256, COLS)
            total = total + jnp.dot(block, w_in[p], preferred_element_type=jnp.float32)
        return total

    mid[...] = product_of(range(6)).reshape(16, GROUP, 4 * FF)
    arrive(passed)
    product = mid[...].reshape(256, 4 * FF) + product_of((6, 7))
    mid[...] = product.reshape(16, GROUP, 4 * FF)
    to_sibling = wires.copy(mid, rx_mid, sibling)
    arrive(mark_copies)
    mark = marks[...].reshape(128, EXT)
    lane = lax.broadcasted_iota(jnp.int32, (128, EXT), 1)

    def mark_at(at):
        low = jnp.sum(jnp.where(lane == at, mark, 0.0), axis=1, keepdims=True)
        high = jnp.sum(jnp.where(lane == at + 32, mark, 0.0), axis=1, keepdims=True)
        both = [low.reshape(16, 1, 8, 1), high.reshape(16, 1, 8, 1)]
        return jnp.concatenate(both, axis=1).reshape(256, 1)

    share, scale = mark_at(e), mark_at(16)
    weigh_tile(0)
    to_sibling.wait_recv()
    hidden = []
    for s in range(16):
        own, other = mid[s], rx_mid[(s % 4) * 4 + s // 4]
        at = scale[s * GROUP : (s + 1) * GROUP]
        g0 = (own[:, 0:FF] + other[:, 2 * FF : 3 * FF]) * at
        u0 = (own[:, FF : 2 * FF] + other[:, 3 * FF : 4 * FF]) * at
        g1 = (own[:, 2 * FF : 3 * FF] + other[:, 0:FF]) * at
        u1 = (own[:, 3 * FF : 4 * FF] + other[:, FF : 2 * FF]) * at
        h0 = bf16(jax.nn.silu(g0) * u0)
        h1 = bf16(jax.nn.silu(g1) * u1)
        hidden.append(jnp.concatenate([h0, h1], axis=1))
    hidden = jnp.concatenate(hidden, axis=0)
    produced = jnp.dot(hidden, w_out[...], preferred_element_type=jnp.float32) * share
    for i in range(8):
        at = jnp.int32(0)
        for p, d in enumerate(PLACES):
            at = jnp.where((z + d - i) % 8 == 0, p, at)
        made_rows[at] = bf16(produced[:, i * COLS : (i + 1) * COLS]).reshape(16, GROUP, COLS)

    early = []
    for step in (2, 1, 3, 0):
        group = pl.ds(((b + step) % 4) * 4, 4)
        for p, d in ((6, 1), (7, -1)):
            src, dst = made_rows.at[p, group], rx_pre.at[p - 6, group]
            early.append(wires.copy(src, dst, place.along_z(d)))
    first, second = [], []

    def sum_b(part, j):
        start, size = SUM_PARTS[part]
        group = pl.ds(((b + RING_STEPS[j]) % 4) * 4, 4)
        src, dst = made_rows.at[pl.ds(start, size), group], rx_b.at[j, pl.ds(start, size)]
        first.append(wires.copy(src, dst, place.plane(a, b + RING_STEPS[j])))

    def sum_a(part):
        start, size = SUM_PARTS[part]
        arrive(first[3 * part : 3 * part + 3])
        at = slice(start, start + size)
        total = f32(made_rows[at, pl.ds(b * 4, 4)])
        for j in range(3):
            total = total + f32(rx_b[j, at])
        mid_b[at] = bf16(total)
        for j, d in enumerate(RING_STEPS):
            src = mid_b.at[pl.ds(start, size), (a + d) % 4]
            dst = rx_a.at[j, pl.ds(start, size)]
            second.append(wires.copy(src, dst, place.plane(a + d, b)))

    for j in range(3):
        sum_b(0, j)
    weigh_tile(1)
    mix_tile(0)
    score_tile(2)
    for j, step in enumerate((2, 1, 3, 0)):
        arrive(early[2 * j : 2 * j + 2])
        group = pl.ds(((b + step) % 4) * 4, 4)
        for i in range(2):
            total = f32(made_rows[4 + i, group]) + f32(rx_pre[i, group])
            made_rows[4 + i, group] = bf16(total)
        if j < 3:
            sum_b(1, j)
    sum_a(0)
    sum_a(1)
    weigh_tile(2)
    mix_tile(1)
    arrive(second)
    total = f32(mid_b[:, a])
    for j in range(3):
        total = total + f32(rx_a[j])
    zsum[...] = bf16(total)
    copies = []
    for p in (5, 4, 3, 2, 1):
        copies.append(wires.copy(zsum.at[p], rx_z2.at[p - 1], place.along_z(PLACES[p])))
    total = residual + total[0]
    mix_tile(2)
    score_tile(3)
    weigh_tile(3)
    arrive(copies)
    for i in range(5):
        total = total + f32(rx_z2[i])
    final[k, z] = bf16(total)
    ref = final.at[k, z]
    copies = [wires.copy(ref, ref, place.along_z(d)) for d in Z_STEPS]
    mix_tile(3)
    for t in range(KVL // 128):
        at = slice(t * 128, (t + 1) * 128)
        pref_rows[:, :, at] = bf16(by_token[t].reshape(TOK, HEADS_DEV, 128))
    pref_copy = pltpu.make_async_copy(pref_rows, pref, load.at[LOADS])
    pref_copy.start()
    arrive(copies)
    to_sibling = wires.copy(final.at[k], final.at[k], sibling)
    to_sibling.wait_recv()
    for i in range(16):
        out[:, i * COLS : (i + 1) * COLS] = final[i // 8, i % 8]
    pref_copy.wait()
    wires.drain()


def layer(*args):
    vmem, smem = pl.BlockSpec(memory_space=VMEM), pl.BlockSpec(memory_space=pltpu.SMEM)
    anywhere = pl.BlockSpec(memory_space=ANY)
    half, full = jnp.bfloat16, jnp.float32
    scratch = [
        ((GROUP, D), half),
        ((D // 128, 128), half),
        ((1, D), full),
        ((16, D), half),
        ((8, GROUP), jnp.int32),
        ((2, 8, TOK, LAT), half),
        ((KVL, 16 * TOK), half),
        ((2, 8, 2 * PAGE, LAT), half),
        ((HEADS_DEV, LAT, TOK), half),
        ((KVL, HEADS_DEV * VD), half),
        ((COLS, HEADS_DEV * VD), half),
        ((8, COLS, 4 * FF), half),
        ((2 * FF, HALF), half),
        ((HEADS_DEV, GROUP * HEADS_DEV, VD), full),
        ((16, GROUP, HEADS_DEV * VD), half),
        ((16, GROUP, COLS), half),
        ((16, GROUP, COLS), half),
        ((8, GROUP, COLS), half),
        ((8, GROUP, COLS), half),
        ((7, GROUP, COLS), half),
        ((8, 16, GROUP, COLS), half),
        ((8, GROUP, EXT), full),
        ((2, GROUP, EXT), full),
        ((16, 8, EXT), full),
        ((KVL // 128, TOK * HEADS_DEV, 128), full),
        ((TOK, HEADS_DEV, KVL), half),
        ((4, 16 * TOK, 2 * TOK), full),
        ((4, 16 * TOK, 2 * TOK), half),
        ((8, 2 * TOK), full),
        ((16, GROUP, 4 * FF), full),
        ((16, GROUP, 4 * FF), full),
        ((8, 16, GROUP, COLS), half),
        ((2, 16, GROUP, COLS), half),
        ((3, 6, 4, GROUP, COLS), half),
        ((6, 4, GROUP, COLS), half),
        ((3, 6, GROUP, COLS), half),
        ((6, GROUP, COLS), half),
        ((5, GROUP, COLS), half),
        ((2, 8, GROUP, COLS), half),
    ]
    return pl.pallas_call(
        layer_kernel,
        out_shape=(
            jax.ShapeDtypeStruct((TOK, HEADS_DEV, KVL), half),
            jax.ShapeDtypeStruct((GROUP, D), half),
        ),
        in_specs=[smem] * 2 + [vmem] * 3 + [anywhere] * 10,
        out_specs=[anywhere, vmem],
        scratch_shapes=[VMEM(shape, dtype) for shape, dtype in scratch]
        + [
            pltpu.SemaphoreType.DMA((COPIES,)),
            pltpu.SemaphoreType.DMA((COPIES,)),
            pltpu.SemaphoreType.DMA((LOADS + 1,)),
        ],
        compiler_params=pltpu.CompilerParams(
            collective_id=1, has_side_effects=True, vmem_limit_bytes=LIMIT
        ),
    )(*args)


def body(
    q_pref,
    kv_pref,
    dec_q,
    dec_kv,
    page_req,
    dec_len,
    w_uv,
    w_o,
    x_dec,
    norm_gain,
    router,
    routes,
    w_gate,
    w_up,
    w_down,
):
    pref, decode_out = layer(
        page_req,
        dec_len,
        kv_pref.T,
        dec_q,
        dec_kv,
        x_dec,
        norm_gain.reshape(D // 128, 128),
        router.T,
        routes.T,
        jnp.transpose(q_pref, (1, 2, 0)),
        w_uv,
        w_o.T,
        w_gate,
        w_up,
        w_down,
    )
    return (pref, decode_out)


def solution(mesh):
    placed = (
        P("ctx", "exp", None),
        P("ctx", None),
        P("exp", "ctx", None),
        P("exp", None),
        P("exp", None),
        P("exp"),
        P("ctx", None, None),
        P("ctx", "exp"),
        P("exp", None),
        P(),
        P(),
        P("exp", None),
        P("exp", None, "ctx"),
        P("exp", None, "ctx"),
        P("exp", "ctx", None),
    )
    return jax.shard_map(
        body,
        mesh=mesh,
        in_specs=placed,
        out_specs=(P("ctx", "exp", None), P("exp", None)),
        check_vma=False,
    )
```

```python
import functools

import jax
import jax.numpy as jnp
from jax import lax
from jax.experimental import pallas as pl
from jax.experimental.pallas import tpu as pltpu
from jax.sharding import PartitionSpec as P

D = 7168
HALF = D // 2
KVL = 512
LAT = 576
HEADS_DEV = 8
VD = 128
FF = 128
TOK = 128
PAGE = 16
GROUP = 16
COLS = 448
EXT = 128
FAR = 1 << 20

qk_scale = 192.0 ** (-0.5)
neg_big = -1e30
MESH = pl.DeviceIdType.MESH
VMEM = pltpu.VMEM
ANY = pl.ANY
LIMIT = 60 * 1024 * 1024


class Place:
    def __init__(self):
        self.c = lax.axis_index("ctx")
        self.e = lax.axis_index("exp")
        self.z, self.k = self.c // 2, self.c % 2
        x, y = self.e // 4, self.e % 4
        self.a = x + self.k * (y - x)
        self.b = y + self.k * (x - y)

    def exp_of(self, a, b):
        return (a + self.k * (b - a)) * 4 + b + self.k * (a - b)

    def plane(self, a, b):
        return (self.c, self.exp_of(a % 4, b % 4))

    def sibling(self):
        return (self.c + 1 - 2 * self.k, self.e)

    def along_z(self, step):
        return (((self.z + step) % 8) * 2 + self.k, self.e)


def greet(devices):
    barrier = pltpu.get_barrier_semaphore()
    for device in devices:
        pl.semaphore_signal(barrier, inc=1, device_id=device, device_id_type=MESH)
    return lambda: pl.semaphore_wait(barrier, len(devices))


class Wires:
    def __init__(self, send_sem, recv_sem):
        self.send_sem, self.recv_sem = send_sem, recv_sem
        self.count = 0
        self.open = []

    def copy(self, src, dst, device):
        i = self.count
        self.count += 1
        made = pltpu.make_async_remote_copy(
            src_ref=src,
            dst_ref=dst,
            send_sem=self.send_sem.at[i],
            recv_sem=self.recv_sem.at[i],
            device_id=device,
            device_id_type=MESH,
        )
        made.start()
        self.open.append(made)
        return made

    def drain(self):
        for made in self.open:
            made.wait_send()
        self.open = []


def arrive(copies):
    for made in copies:
        made.wait_recv()


def f32(value):
    return value.astype(jnp.float32)


def bf16(value):
    return value.astype(jnp.bfloat16)


Z_STEPS = (4, 3, -3, 2, -2, 1, -1)
PLANE_STEPS = (
    (2, 2), (2, 1), (2, 3), (1, 2), (3, 2), (1, 1), (1, 3), (3, 1), (3, 3),
    (2, 0), (0, 2), (1, 0), (3, 0), (0, 1), (0, 3),
)
RING_STEPS = (2, 1, 3)
PLACES = (0, 1, -1, -2, 2, -3, 3, 4)
PARTS = ((4, 2), (0, 4))
SUM_PARTS = ((0, 4), (4, 2))
COPIES = 7 + 1 + 17 + 17 + 15 + 15 + 1 + 7 + 12 + 30 + 8 + 1 + 15 + 1 + 8 + 12 + 5 + 7 + 1
LOADS = HEADS_DEV + 5 + 16 + 1 + 1


def layer_kernel(
    pages, lengths, kv_t, dec_q, dec_kv,
    x_dec_in, gain_in, router_in, routes_in, q_t, w_uv, w_o_t, gate, up, down,
    pref, out,
    x_dec, gain_rows, gain, router_t, routes, keys, keys_t, cache, v_q, v_uv, v_o, w_in, w_out, latent, vals, parts, blocks, rx_half, red, rx_z,
    rows, sums, rx_sums, marks, by_token, pref_rows, scores_at, weights_at, totals, mid, rx_mid, made_rows, rx_pre, rx_b, mid_b, rx_a,
    zsum, rx_z2, final, send, recv, load,
):
    place = Place()
    z, k, a, b, c, e = place.z, place.k, place.a, place.b, place.c, place.e
    sibling = place.sibling()
    half = pl.ds(k * HALF, HALF)
    other_half = pl.ds((1 - k) * HALF, HALF)
    def block_copies(side, at):
        pairs = []
        for p, d in enumerate(PLACES):
            block = pl.ds((side * 8 + (z + d) % 8) * COLS, COLS)
            pairs.append((gate.at[0, block, :], w_in.at[p, :, pl.ds(at * FF, FF)]))
            pairs.append((up.at[0, block, :], w_in.at[p, :, pl.ds((at + 1) * FF, FF)]))
        return pairs

    enter = greet(
        [sibling]
        + [place.along_z(d) for d in Z_STEPS]
        + [place.plane(a + i, b + j) for i, j in PLANE_STEPS]
    )
    loads = []
    for i, (src, dst) in enumerate(
        [(w_uv.at[h], v_uv.at[:, pl.ds(h * VD, VD)]) for h in range(HEADS_DEV)]
        + [
            (w_o_t, v_o),
            (x_dec_in, x_dec),
            (gain_in, gain_rows),
            (router_in, router_t),
            (routes_in, routes),
        ]
        + block_copies(k, 0)
        + [(down.at[0, :, half], w_out.at[pl.ds(0, FF), :]), (q_t, v_q)]
    ):
        made = pltpu.make_async_copy(src, dst, load.at[i])
        made.start()
        loads.append(made)
    keys[k, z] = jnp.transpose(kv_t[...])

    source = [pages[0, i] // 8 for i in range(16)]
    rank = []
    for i in range(16):
        before = jnp.int32(0)
        for j in range(i):
            before = before + jnp.where(source[j] == source[i], 1, 0)
        rank.append(before)
    for j in range(2):
        wanted = jnp.int32(0)
        for i in range(16):
            wanted = jnp.where((source[i] == c) & (rank[i] == j), pages[0, i] % 8, wanted)
        page = keys[k, z, 0:PAGE, :]
        for i in range(1, 8):
            page = jnp.where(wanted == i, keys[k, z, i * PAGE : (i + 1) * PAGE, :], page)
        cache[k, z, j * PAGE : (j + 1) * PAGE, :] = page

    enter()
    wires = Wires(send, recv)
    mine = cache.at[k, z]
    page_copies = [wires.copy(mine, mine, place.along_z(d)) for d in Z_STEPS]
    swaps = [wires.copy(src, dst, sibling) for src, dst in block_copies(1 - k, 2)]
    swaps.append(wires.copy(down.at[0, :, other_half], w_out.at[pl.ds(FF, FF), :], sibling))

    count = HEADS_DEV * GROUP
    queries = dec_q[...].reshape(count, LAT)
    own = jnp.broadcast_to(f32(dec_kv[...])[:, None, :], (GROUP, HEADS_DEV, LAT))
    own = own.reshape(count, LAT)
    own_score = jnp.sum(f32(queries) * own, axis=1, keepdims=True)
    row = lax.broadcasted_iota(jnp.int32, (count, 1), 0) // HEADS_DEV
    limit = jnp.zeros((count, 1), jnp.int32)
    for i in range(GROUP):
        limit = jnp.where(row == i, lengths[i], limit)
    lane = lax.broadcasted_iota(jnp.int32, (1, 256), 1)
    allowed = []
    for core in (k, 1 - k):
        position = jnp.full((1, 256), FAR, jnp.int32)
        for i in range(16):
            here = ((lane // 32) * 2 + core == source[i]) & ((lane // PAGE) % 2 == rank[i])
            position = jnp.where(here, i * PAGE + lane % PAGE, position)
        allowed.append(position < limit)
    arrive(page_copies)
    to_sibling = wires.copy(cache.at[k], cache.at[k], sibling)
    block = keys.at[k, z]
    to_r = wires.copy(block, block, place.along_z(1))
    to_l = wires.copy(block, block, place.along_z(-1))
    key_copies = [wires.copy(block, block, sibling)]

    def ring_hop(hop, to_r, to_l):
        to_r.wait_recv()
        to_l.wait_recv()
        if hop == 4:
            ref = keys.at[k, (z + 4) % 8]
            key_copies.append(wires.copy(ref, ref, sibling))
            return None, None
        first, second = keys.at[k, (z - hop) % 8], keys.at[k, (z + hop) % 8]
        right, left = first, second
        if hop == 3:
            right = keys.at[k, (z - hop) % 8, pl.ds(0, TOK // 2), :]
            left = keys.at[k, (z + hop) % 8, pl.ds(TOK // 2, TOK // 2), :]
        to_r = wires.copy(right, right, place.along_z(1))
        to_l = wires.copy(left, left, place.along_z(-1))
        key_copies.append(wires.copy(first, first, sibling))
        key_copies.append(wires.copy(second, second, sibling))
        return to_r, to_l

    scores = []
    for i, core in enumerate((k, 1 - k)):
        if i == 1:
            to_sibling.wait_recv()
        cached = cache[core].reshape(256, LAT)
        score = lax.dot_general(
            queries, cached, (((1,), (1,)), ((), ())), preferred_element_type=jnp.float32
        )
        scores.append(jnp.where(allowed[i], score, neg_big))
    top = jnp.maximum(jnp.max(scores[0], axis=1, keepdims=True), own_score)
    top = jnp.maximum(jnp.max(scores[1], axis=1, keepdims=True), top)
    own_weight = jnp.exp((own_score - top) * qk_scale)
    total = own_weight
    mixed = f32(bf16(own_weight)) * own[:, :KVL]
    for i, core in enumerate((k, 1 - k)):
        weights = jnp.where(allowed[i], jnp.exp((scores[i] - top) * qk_scale), 0.0)
        total = total + jnp.sum(weights, axis=1, keepdims=True)
        cached = cache[core].reshape(256, LAT)
        mixed = mixed + jnp.dot(
            bf16(weights), cached[:, :KVL], preferred_element_type=jnp.float32
        )
    for made in loads[:HEADS_DEV]:
        made.wait()
    product = jnp.dot(bf16(mixed / total), v_uv[...], preferred_element_type=jnp.float32)
    for h in range(HEADS_DEV):
        latent[h] = product[:, h * VD : (h + 1) * VD]
        part = latent[h, pl.ds(h, GROUP, stride=HEADS_DEV), :]
        vals[e, :, h * VD : (h + 1) * VD] = bf16(part)

    near = [place.plane(a + i, b + j) for i, j in PLANE_STEPS]
    copies = [wires.copy(vals.at[e], vals.at[e], device) for device in near]
    to_r, to_l = ring_hop(1, to_r, to_l)
    for made in loads[HEADS_DEV : HEADS_DEV + 5]:
        made.wait()
    for i in range(D // 128):
        gain[:, i * 128 : (i + 1) * 128] = f32(gain_rows[i : i + 1, :])
    arrive(copies)
    product = lax.dot_general(
        vals[...].reshape(256, HEADS_DEV * VD),
        v_o[...],
        (((1,), (1,)), ((), ())),
        preferred_element_type=jnp.float32,
    )
    parts[...] = bf16(product).reshape(16, GROUP, COLS)
    copies = [wires.copy(parts.at[device[1]], blocks.at[e], device) for device in near]
    blocks[e] = parts[e]
    to_r, to_l = ring_hop(2, to_r, to_l)
    arrive(copies)
    to_sibling = wires.copy(blocks.at[pl.ds((1 - k) * 8, 8)], rx_half, sibling)
    to_sibling.wait_recv()
    red[...] = bf16(f32(blocks[pl.ds(k * 8, 8)]) + f32(rx_half[...]))

    def sum_z(ref, rx, meanwhile):
        copies = []
        for i, d in enumerate(Z_STEPS):
            copies.append(wires.copy(ref.at[(z + d) % 8], rx.at[i], place.along_z(d)))
        total = f32(ref[z])
        meanwhile()
        for i in range(7):
            copies[i].wait_recv()
            total = total + f32(rx[i])
        return total

    pair = pl.ds((k * 4 + z // 2) * 2 * COLS, 2 * COLS)
    odd = z % 2 == 1
    x_pair, gain_pair, router_pair = f32(x_dec[:, pair]), gain[:, pair], f32(router_t[:, pair])
    x_own = jnp.where(odd, x_pair[:, COLS:], x_pair[:, :COLS])
    gain_own = jnp.where(odd, gain_pair[:, COLS:], gain_pair[:, :COLS])
    router_own = jnp.where(odd, router_pair[:, COLS:], router_pair[:, :COLS])
    ring = []
    residual = x_own + sum_z(red, rx_z, lambda: ring.extend(ring_hop(3, to_r, to_l)))
    scaled = bf16(residual * gain_own)
    slot = b * 4 + a
    rows[0, slot] = scaled
    spread = {}
    for p in (5, 4, 3, 1, 2):
        spread[p] = wires.copy(rows.at[0, slot], rows.at[p, slot], place.along_z(-PLACES[p]))

    ring_hop(4, *ring)

    lane = lax.broadcasted_iota(jnp.int32, (GROUP, EXT), 1)
    sums[z, :, 0:16] = lax.dot_general(
        scaled, bf16(router_own), (((1,), (1,)), ((), ())), preferred_element_type=jnp.float32
    )
    squares = jnp.sum(residual * residual, axis=1, keepdims=True)
    sums[z, :, 16:EXT] = jnp.broadcast_to(squares, (GROUP, EXT - 16))

    along_a, along_b = [], []

    def send_part(part):
        first, size = PARTS[part]
        for p in range(first, first + size):
            if p > 0:
                spread[p].wait_recv()
        ref = rows.at[pl.ds(first, size), slot]
        along_a.append([wires.copy(ref, ref, place.plane(a + d, b)) for d in RING_STEPS])
        along_b.append([wires.copy(ref, ref, place.plane(a, b + d)) for d in RING_STEPS])

    def pass_part(part):
        first, size = PARTS[part]
        for i, d in zip((1, 2, 0), (1, 3, 2)):
            along_a[part][i].wait_recv()
            ref = rows.at[pl.ds(first, size), b * 4 + (a - d) % 4]
            along_b[part] += [wires.copy(ref, ref, place.plane(a, b + j)) for j in RING_STEPS]

    passed = []

    def pass_z(j):
        group = pl.ds(((b + j) % 4) * 4, 4)
        for p, q, d in ((4, 6, -1), (5, 7, 1)):
            passed.append(wires.copy(rows.at[p, group], rows.at[q, group], place.along_z(d)))

    def pass_z_from(step):
        arrive(along_b[0][RING_STEPS.index(step) :: 3])
        pass_z(-step)

    send_part(0)
    send_part(1)
    sum_copies = [wires.copy(sums.at[z], sums.at[z], place.along_z(d)) for d in Z_STEPS]
    arrive(key_copies)
    for i in range(16):
        block = keys[i // 8, i % 8, :, 0:KVL]
        keys_t[:, i * TOK : (i + 1) * TOK] = jnp.transpose(block)
    loads[-1].wait()
    pass_part(0)
    pass_z(0)
    pass_part(1)
    arrive(sum_copies)
    total = sums[0]
    for i in range(1, 8):
        total = total + sums[i]
    rx_sums[k] = total
    to_sibling = wires.copy(rx_sums.at[k], rx_sums.at[k], sibling)
    pass_z_from(1)
    pass_z_from(3)
    to_sibling.wait_recv()
    both = rx_sums[0] + rx_sums[1]
    scale = lax.rsqrt(both[:, 16:17] / D + 1e-06)
    affinity = jax.nn.sigmoid(both * scale)
    itself = lax.broadcasted_iota(jnp.int32, (GROUP, GROUP), 0) == lax.broadcasted_iota(
        jnp.int32, (GROUP, GROUP), 1
    )
    chosen = lane < 0
    for t in range(routes.shape[0]):
        named = jnp.sum(jnp.where(itself, routes[t : t + 1, :], 0), axis=1, keepdims=True)
        chosen = chosen | (lane == named)
    picked = jnp.where(chosen, affinity, 0.0)
    share = 2.5 * picked / jnp.sum(picked, axis=1, keepdims=True)
    mark = jnp.where(lane == 16, scale, share)
    marks[slot] = jnp.where(lane[0:8] < 32, mark[0:8], pltpu.roll(mark[8:16], 32, 1))
    mark_copies = [wires.copy(marks.at[slot], marks.at[slot], device) for device in near]
    pass_z_from(2)
    def score_tile(i):
        queries = jnp.concatenate([v_q[2 * i], v_q[2 * i + 1]], axis=1)
        scores_at[i] = jnp.dot(
            keys[...].reshape(16 * TOK, LAT), queries, preferred_element_type=jnp.float32
        )

    def weigh_tile(i):
        shape = (TOK, 2 * TOK)
        ahead = lax.broadcasted_iota(jnp.int32, shape, 0)
        ahead = ahead - lax.broadcasted_iota(jnp.int32, shape, 1) % TOK

        def block(n):
            behind = (c - (n % 8) * 2 - n // 8) * TOK
            return jnp.where(ahead <= behind, scores_at[i, n * TOK : (n + 1) * TOK], neg_big)

        top = block(0)
        for n in range(1, 16):
            top = jnp.maximum(top, block(n))
        top = jnp.max(top, axis=0, keepdims=True)
        total = 0.0
        for n in range(16):
            weights = jnp.exp((block(n) - top) * qk_scale)
            total = total + weights
            weights_at[i, n * TOK : (n + 1) * TOK] = bf16(weights)
        totals[i : i + 1] = jnp.sum(total, axis=0, keepdims=True)

    def mix_tile(i):
        mixed = jnp.dot(keys_t[...], weights_at[i], preferred_element_type=jnp.float32)
        mixed = mixed / totals[i : i + 1]
        for j in range(2):
            head = jnp.transpose(mixed[:, j * TOK : (j + 1) * TOK])
            every = pl.ds(2 * i + j, TOK, stride=HEADS_DEV)
            for t in range(KVL // 128):
                by_token[t, every, :] = head[:, t * 128 : (t + 1) * 128]

    score_tile(0)
    score_tile(1)
    arrive(along_b[1])
    for made in loads[HEADS_DEV + 5 : -1]:
        made.wait()
    arrive(swaps)

    def product_of(places):
        total = 0.0
        for p in places:
            block = rows[p].reshape(256, COLS)
            total = total + jnp.dot(block, w_in[p], preferred_element_type=jnp.float32)
        return total

    mid[...] = product_of(range(6)).reshape(16, GROUP, 4 * FF)
    arrive(passed)
    product = mid[...].reshape(256, 4 * FF) + product_of((6, 7))
    mid[...] = product.reshape(16, GROUP, 4 * FF)
    to_sibling = wires.copy(mid, rx_mid, sibling)
    arrive(mark_copies)
    mark = marks[...].reshape(128, EXT)
    lane = lax.broadcasted_iota(jnp.int32, (128, EXT), 1)

    def mark_at(at):
        low = jnp.sum(jnp.where(lane == at, mark, 0.0), axis=1, keepdims=True)
        high = jnp.sum(jnp.where(lane == at + 32, mark, 0.0), axis=1, keepdims=True)
        both = [low.reshape(16, 1, 8, 1), high.reshape(16, 1, 8, 1)]
        return jnp.concatenate(both, axis=1).reshape(256, 1)

    share, scale = mark_at(e), mark_at(16)
    weigh_tile(0)
    to_sibling.wait_recv()
    hidden = []
    for s in range(16):
        own, other = mid[s], rx_mid[(s % 4) * 4 + s // 4]
        at = scale[s * GROUP : (s + 1) * GROUP]
        g0 = (own[:, 0:FF] + other[:, 2 * FF : 3 * FF]) * at
        u0 = (own[:, FF : 2 * FF] + other[:, 3 * FF : 4 * FF]) * at
        g1 = (own[:, 2 * FF : 3 * FF] + other[:, 0:FF]) * at
        u1 = (own[:, 3 * FF : 4 * FF] + other[:, FF : 2 * FF]) * at
        h0 = bf16(jax.nn.silu(g0) * u0)
        h1 = bf16(jax.nn.silu(g1) * u1)
        hidden.append(jnp.concatenate([h0, h1], axis=1))
    hidden = jnp.concatenate(hidden, axis=0)
    produced = jnp.dot(hidden, w_out[...], preferred_element_type=jnp.float32) * share
    for i in range(8):
        at = jnp.int32(0)
        for p, d in enumerate(PLACES):
            at = jnp.where((z + d - i) % 8 == 0, p, at)
        made_rows[at] = bf16(produced[:, i * COLS : (i + 1) * COLS]).reshape(16, GROUP, COLS)

    early = []
    for step in (2, 1, 3, 0):
        group = pl.ds(((b + step) % 4) * 4, 4)
        for p, d in ((6, 1), (7, -1)):
            src, dst = made_rows.at[p, group], rx_pre.at[p - 6, group]
            early.append(wires.copy(src, dst, place.along_z(d)))
    first, second = [], []

    def sum_b(part, j):
        start, size = SUM_PARTS[part]
        group = pl.ds(((b + RING_STEPS[j]) % 4) * 4, 4)
        src, dst = made_rows.at[pl.ds(start, size), group], rx_b.at[j, pl.ds(start, size)]
        first.append(wires.copy(src, dst, place.plane(a, b + RING_STEPS[j])))

    def sum_a(part):
        start, size = SUM_PARTS[part]
        arrive(first[3 * part : 3 * part + 3])
        at = slice(start, start + size)
        total = f32(made_rows[at, pl.ds(b * 4, 4)])
        for j in range(3):
            total = total + f32(rx_b[j, at])
        mid_b[at] = bf16(total)
        for j, d in enumerate(RING_STEPS):
            src = mid_b.at[pl.ds(start, size), (a + d) % 4]
            dst = rx_a.at[j, pl.ds(start, size)]
            second.append(wires.copy(src, dst, place.plane(a + d, b)))

    for j in range(3):
        sum_b(0, j)
    weigh_tile(1)
    mix_tile(0)
    score_tile(2)
    for j, step in enumerate((2, 1, 3, 0)):
        arrive(early[2 * j : 2 * j + 2])
        group = pl.ds(((b + step) % 4) * 4, 4)
        for i in range(2):
            total = f32(made_rows[4 + i, group]) + f32(rx_pre[i, group])
            made_rows[4 + i, group] = bf16(total)
        if j < 3:
            sum_b(1, j)
    sum_a(0)
    sum_a(1)
    weigh_tile(2)
    mix_tile(1)
    arrive(second)
    total = f32(mid_b[:, a])
    for j in range(3):
        total = total + f32(rx_a[j])
    zsum[...] = bf16(total)
    copies = []
    for p in (5, 4, 3, 2, 1):
        copies.append(wires.copy(zsum.at[p], rx_z2.at[p - 1], place.along_z(PLACES[p])))
    total = residual + total[0]
    mix_tile(2)
    score_tile(3)
    weigh_tile(3)
    arrive(copies)
    for i in range(5):
        total = total + f32(rx_z2[i])
    final[k, z] = bf16(total)
    ref = final.at[k, z]
    copies = [wires.copy(ref, ref, place.along_z(d)) for d in Z_STEPS]
    mix_tile(3)
    for t in range(KVL // 128):
        at = slice(t * 128, (t + 1) * 128)
        pref_rows[:, :, at] = bf16(by_token[t].reshape(TOK, HEADS_DEV, 128))
    pref_copy = pltpu.make_async_copy(pref_rows, pref, load.at[LOADS])
    pref_copy.start()
    arrive(copies)
    to_sibling = wires.copy(final.at[k], final.at[k], sibling)
    to_sibling.wait_recv()
    for i in range(16):
        out[:, i * COLS : (i + 1) * COLS] = final[i // 8, i % 8]
    pref_copy.wait()
    wires.drain()


def layer(*args):
    vmem, smem = pl.BlockSpec(memory_space=VMEM), pl.BlockSpec(memory_space=pltpu.SMEM)
    anywhere = pl.BlockSpec(memory_space=ANY)
    half, full = jnp.bfloat16, jnp.float32
    scratch = [
        ((GROUP, D), half),
        ((D // 128, 128), half),
        ((1, D), full),
        ((16, D), half),
        ((8, GROUP), jnp.int32),
        ((2, 8, TOK, LAT), half),
        ((KVL, 16 * TOK), half),
        ((2, 8, 2 * PAGE, LAT), half),
        ((HEADS_DEV, LAT, TOK), half),
        ((KVL, HEADS_DEV * VD), half),
        ((COLS, HEADS_DEV * VD), half),
        ((8, COLS, 4 * FF), half),
        ((2 * FF, HALF), half),
        ((HEADS_DEV, GROUP * HEADS_DEV, VD), full),
        ((16, GROUP, HEADS_DEV * VD), half),
        ((16, GROUP, COLS), half),
        ((16, GROUP, COLS), half),
        ((8, GROUP, COLS), half),
        ((8, GROUP, COLS), half),
        ((7, GROUP, COLS), half),
        ((8, 16, GROUP, COLS), half),
        ((8, GROUP, EXT), full),
        ((2, GROUP, EXT), full),
        ((16, 8, EXT), full),
        ((KVL // 128, TOK * HEADS_DEV, 128), full),
        ((TOK, HEADS_DEV, KVL), half),
        ((4, 16 * TOK, 2 * TOK), full),
        ((4, 16 * TOK, 2 * TOK), half),
        ((8, 2 * TOK), full),
        ((16, GROUP, 4 * FF), full),
        ((16, GROUP, 4 * FF), full),
        ((8, 16, GROUP, COLS), half),
        ((2, 16, GROUP, COLS), half),
        ((3, 6, 4, GROUP, COLS), half),
        ((6, 4, GROUP, COLS), half),
        ((3, 6, GROUP, COLS), half),
        ((6, GROUP, COLS), half),
        ((5, GROUP, COLS), half),
        ((2, 8, GROUP, COLS), half),
    ]
    return pl.pallas_call(
        layer_kernel,
        out_shape=(
            jax.ShapeDtypeStruct((TOK, HEADS_DEV, KVL), half),
            jax.ShapeDtypeStruct((GROUP, D), half),
        ),
        in_specs=[smem] * 2 + [vmem] * 3 + [anywhere] * 10,
        out_specs=[anywhere, vmem],
        scratch_shapes=[VMEM(shape, dtype) for shape, dtype in scratch]
        + [
            pltpu.SemaphoreType.DMA((COPIES,)),
            pltpu.SemaphoreType.DMA((COPIES,)),
            pltpu.SemaphoreType.DMA((LOADS + 1,)),
        ],
        compiler_params=pltpu.CompilerParams(
            collective_id=1, has_side_effects=True, vmem_limit_bytes=LIMIT
        ),
    )(*args)


def hand_out_kernel(pref_in, out_in, pref, out, sem):
    copies = [
        pltpu.make_async_copy(pref_in, pref, sem.at[0]),
        pltpu.make_async_copy(out_in, out, sem.at[1]),
    ]
    for made in copies:
        made.start()
    for made in copies:
        made.wait()


def hand_out(pref, out):
    return pl.pallas_call(
        hand_out_kernel,
        out_shape=tuple(jax.ShapeDtypeStruct(x.shape, x.dtype) for x in (pref, out)),
        in_specs=[pl.BlockSpec(memory_space=VMEM)] * 2,
        out_specs=[pl.BlockSpec(memory_space=ANY)] * 2,
        scratch_shapes=[pltpu.SemaphoreType.DMA((2,))],
    )(pref, out)


def body(
    q_pref,
    kv_pref,
    dec_q,
    dec_kv,
    page_req,
    dec_len,
    w_uv,
    w_o,
    x_dec,
    norm_gain,
    router,
    routes,
    w_gate,
    w_up,
    w_down,
):
    pref, decode_out = layer(
        page_req,
        dec_len,
        kv_pref.T,
        dec_q,
        dec_kv,
        x_dec,
        norm_gain.reshape(D // 128, 128),
        router.T,
        routes.T,
        jnp.transpose(q_pref, (1, 2, 0)),
        w_uv,
        w_o.T,
        w_gate,
        w_up,
        w_down,
    )
    return hand_out(pref, decode_out)


def solution(mesh):
    placed = (
        P("ctx", "exp", None),
        P("ctx", None),
        P("exp", "ctx", None),
        P("exp", None),
        P("exp", None),
        P("exp"),
        P("ctx", None, None),
        P("ctx", "exp"),
        P("exp", None),
        P(),
        P(),
        P("exp", None),
        P("exp", None, "ctx"),
        P("exp", None, "ctx"),
        P("exp", "ctx", None),
    )
    return jax.shard_map(
        body,
        mesh=mesh,
        in_specs=placed,
        out_specs=(P("ctx", "exp", None), P("exp", None)),
        check_vma=False,
    )
```
